256 devices in a mesh: dp: 32 (over z, y), freq: 8 (over x, core).
Axes of the slice: x: 4, y: 4, z: 8, core: 2. Of those that a mesh axis runs over, the one named last changes fastest.
Arguments:
- inputs: bfloat16 [32768, 128], P('dp'), may hold values from -6 to 6
- freqs: bfloat16 [128, 32768], P(None, 'freq'), may hold values from -1.5 to 1.5
- targets: bfloat16 [32768, 64], P('dp'), may hold values from -6 to 6
- counts: int32 [32], P('dp'), may hold values from 256 to 1024, as said below
Outputs:
- weights: float32 [2, 32768, 64], P(None, 'freq')
The draws below stay inside these ranges and needn't reach their ends.
Inputs may be any that keep to these rules, and one draw needn't show every extreme that they name: `counts`: some index of dp has all 1024 slots valid and some has a quarter of them.
All inputs are finite; a program needn't handle non-finite values.
Results may differ from the reference program's by a relative error of at most 0.0031.
Values may be sent and summed in bfloat16 or wider, within the bound.
A program may use at most 64 MiB of HBM per device.

```python
import jax
import jax.numpy as jnp
from jax import lax

D_IN = 128
PAIRS = 32768
TARGETS = 64
ROWS_DEV = 1024
ITERS = 2
SAMPLES = 32768
N_DP = 32


def draw_counts(key, part):
    key = jax.random.fold_in(key, 11)
    first, second = jax.random.split(key)
    base = jax.random.randint(first, (N_DP,), ROWS_DEV // 4, ROWS_DEV + 1)
    order = jax.random.permutation(second, N_DP)
    slots = jnp.arange(N_DP)
    base = jnp.where(slots == order[0], ROWS_DEV, base)
    base = jnp.where(slots == order[1], ROWS_DEV // 4, base)
    return base.astype(jnp.int32)


def block_levels(rng, extent, cuts, smallest, high):
    def one(axis_at, blocks):
        steps = jax.random.uniform(jax.random.fold_in(jax.random.fold_in(rng, 6), axis_at), (blocks,), jnp.float32, smallest / len(cuts), high / len(cuts))
        return jnp.repeat(jnp.exp(steps), extent[axis_at] // blocks).reshape((-1,) + (1,) * (len(extent) - axis_at - 1))

    gain = one(*cuts[0])
    for cut in cuts[1:]:
        gain = gain * one(*cut)
    return gain


def gaussian(own_key, dims, scale, limit, shards=(), held_as=jnp.bfloat16):
    drawn = jax.random.normal(own_key, dims, jnp.float32) * scale
    if len(shards) > 0:
        drawn = block_levels(own_key, dims, shards, -0.22, 0.18) * drawn
    return jnp.clip(drawn, min=-limit, max=limit).astype(held_as)


def setup_inputs(seed: int = 0) -> dict:
    key_of = jax.random.split(jax.random.key(seed), 5)
    inputs = gaussian(key_of[0], (SAMPLES, D_IN), 1.0, 6.0, ((0, 32),))
    freqs = gaussian(key_of[1], (D_IN, PAIRS), 16 ** -0.5, 1.5, ((1, 8),))
    targets = gaussian(key_of[2], (SAMPLES, TARGETS), 1.0, 6.0, ((0, 32),))
    counts = draw_counts(jax.random.fold_in(key_of[4], 71), 0)
    return {"inputs": inputs, "freqs": freqs, "targets": targets, "counts": counts}


RIDGE = 0.5


def block_tile(x_block, freqs, count):
    phase = jnp.dot(x_block, freqs, preferred_element_type=jnp.float32)
    slots = jnp.arange(ROWS_DEV, dtype=jnp.int32)
    live = (slots < count).astype(jnp.float32)[:, None] * (PAIRS ** -0.5)
    return jnp.stack([jnp.cos(phase) * live, jnp.sin(phase) * live]).astype(jnp.bfloat16)


def apply_normal(direction, inputs, freqs, counts):
    low = direction.astype(jnp.bfloat16).astype(jnp.float32)
    blocks = inputs.reshape(N_DP, ROWS_DEV, D_IN)

    def step(total, item):
        x_block, count = item
        tile = block_tile(x_block, freqs, count).astype(jnp.float32)
        images = jnp.einsum('crp,cpk->rk', tile, low).astype(jnp.bfloat16).astype(jnp.float32)
        return total + jnp.einsum('crp,rk->cpk', tile, images), None

    total, unused = lax.scan(step, jnp.zeros(direction.shape, jnp.float32), (blocks, counts))
    return total + RIDGE * direction


def right_side(inputs, freqs, targets, counts):
    blocks = inputs.reshape(N_DP, ROWS_DEV, D_IN)
    values = targets.reshape(N_DP, ROWS_DEV, TARGETS)

    def step(total, item):
        x_block, y_block, count = item
        tile = block_tile(x_block, freqs, count).astype(jnp.float32)
        return total + jnp.einsum('crp,rk->cpk', tile, y_block.astype(jnp.float32)), None

    total, unused = lax.scan(step, jnp.zeros((2, PAIRS, TARGETS), jnp.float32), (blocks, values, counts))
    return total


def reference(inputs, freqs, targets, counts):
    right = right_side(inputs, freqs, targets, counts)
    weights = jnp.zeros_like(right)
    residual = right
    direction = right
    norm_now = jnp.sum(residual * residual, axis=(0, 1))
    for step in range(ITERS):
        image = apply_normal(direction, inputs, freqs, counts)
        alpha = norm_now / jnp.sum(direction * image, axis=(0, 1))
        weights = weights + alpha * direction
        residual = residual - alpha * image
        fresh = jnp.sum(residual * residual, axis=(0, 1))
        direction = residual + (fresh / norm_now) * direction
        norm_now = fresh
    return weights
```

```python
import functools
import math

import jax
import jax.numpy as jnp
from jax import lax
from jax.experimental import pallas as pl
from jax.experimental.pallas import tpu as pltpu
from jax.sharding import PartitionSpec as P

MESH = pl.DeviceIdType.MESH
RIDGE = 0.5
NY = 4
ROWT = 128

SIN_HALF = (3.14159258, -5.16770687, 2.55003119, -0.598044194, 0.0772183862)
COS_HALF = (0.999999953, -4.93479283, 4.05841135, -1.33187657, 0.219689611)
INV_TURN = 0.15915494309189535


def nt_dot(a, b):
    return lax.dot_general(a, b, (((1,), (1,)), ((), ())), preferred_element_type=jnp.float32)


def cos_sin(phase, scale):
    gain = math.sqrt(2.0 * scale)
    turns = phase * INV_TURN
    frac = turns - jnp.round(turns)
    sq = frac * frac
    s = SIN_HALF[4] * gain
    c = COS_HALF[4] * gain
    for i in (3, 2, 1, 0):
        s = s * sq + SIN_HALF[i] * gain
        c = c * sq + COS_HALF[i] * gain
    s = s * frac
    return scale - s * s, s * c


def kernel(nz, nf, scale, count_ref, x_ref, w_ref, y_ref, out_ref, s):
    rows = 128 * nf
    f32, bf16 = jnp.float32, jnp.bfloat16
    dp, me = lax.axis_index("dp"), lax.axis_index("freq")
    z, y = dp // NY, dp % NY
    p1, p2, far = y + 1 - 2 * (y % 2), 3 - y, (y + 2) % NY
    count = count_ref[0]
    T, ph, acc = s["T"], s["ph"], s["acc"]

    def at_y(v):
        return (z * NY + v, me)

    def at_z(v):
        return (v * NY + y, me)

    def at_f(v):
        return (dp, v)

    barrier = pltpu.get_barrier_semaphore()
    peers = [at_y((y + d) % NY) for d in range(1, NY)]
    peers += [at_z((z + d) % nz) for d in range(1, nz)]
    peers += [at_f((me + d) % nf) for d in range(1, nf)]
    for peer in peers:
        pl.semaphore_signal(barrier, inc=1, device_id=peer, device_id_type=MESH)

    started = []
    used = [0]

    def push(src, dst, peer):
        k = used[0]
        used[0] += 1
        copy = pltpu.make_async_remote_copy(
            src_ref=src, dst_ref=dst, send_sem=s["send"].at[k], recv_sem=s["recv"].at[k],
            device_id=peer, device_id_type=MESH)
        copy.start()
        started.append(copy)
        return copy

    lane = lax.broadcasted_iota(jnp.int32, (64, rows), 1)
    s["yb"][...] = jnp.where(lane < count, y_ref[...].astype(f32), 0.0).astype(bf16)

    def features(yd):
        def block(j, _):
            chunk = yd * nz + 2 * j
            off = pl.multiple_of(chunk * 128, 128)
            ph[...] = jnp.dot(x_ref[...], w_ref[:, pl.ds(off, 256)], preferred_element_type=f32)

            def tile(i, _):
                r = pl.ds(pl.multiple_of(i * ROWT, ROWT), ROWT)
                c, v = cos_sin(ph[r, :], scale)
                c, v = c.astype(bf16), v.astype(bf16)
                for h in range(2):
                    T[chunk + h, r, 0:128] = c[:, 128 * h:128 * h + 128]
                    T[chunk + h, r, 128:256] = v[:, 128 * h:128 * h + 128]
                return 0

            lax.fori_loop(0, rows // ROWT, tile, 0)
            return 0

        lax.fori_loop(0, nz // 2, block, 0)

    def back(yd, rhs, own, low):
        step = min(4, nz)

        def block(j, _):
            for h in range(step):
                zd = step * j + h
                v = jnp.dot(rhs[...], T[yd * nz + zd], preferred_element_type=f32)
                for c in range(2):
                    own[c, yd, zd] = v[:, 128 * c:128 * c + 128]
                    if low is not None:
                        low[c, yd, zd] = v[:, 128 * c:128 * c + 128].astype(bf16)
            return 0

        lax.fori_loop(0, nz // step, block, 0)

    def back_reduce(tag, rhs, with_features):
        own, low = s["own"], None
        if tag == "g":
            low = s["low"]
        out = own if low is None else low
        r1, r2, st, tot, zr = (s[k + tag] for k in ("r1", "r2", "st", "tot", "zr"))
        kind = st.dtype

        def group(yd):
            if with_features:
                features(yd)
            back(yd, rhs, own, low)

        def fold(c, yd, got):
            def add(i, _):
                st[c, i] = (own[c, yd, i] + r1[c, 0, i].astype(f32)).astype(kind)
                return 0

            lax.fori_loop(0, nz, add, 0)

        group(far)
        if with_features:
            pl.semaphore_wait(barrier, len(peers))
        a0 = push(out.at[0, far], r1.at[0, 0], at_y(p1))
        b0 = push(out.at[1, far], r1.at[1, 0], at_y(p2))
        group(p1)
        a1 = push(out.at[0, p1], r1.at[0, 1], at_y(p1))
        b0.wait_recv()
        fold(1, p1, b0)
        b2 = push(st.at[1], r2.at[1], at_y(p1))
        group(p2)
        b1 = push(out.at[1, p2], r1.at[1, 1], at_y(p2))
        a0.wait_recv()
        fold(0, p2, a0)
        a2 = push(st.at[0], r2.at[0], at_y(p2))
        group(y)
        for copy in (a1, b2, b1, a2):
            copy.wait_recv()

        def total(zd):
            return [own[c, y, zd] + r1[c, 1, zd].astype(f32) + r2[c, zd].astype(f32) for c in range(2)]

        arriving = []
        for d in range(1, nz):
            zd = (z + d) % nz
            for c, v in enumerate(total(zd)):
                tot[d, c] = v.astype(kind)
            arriving.append(push(tot.at[d], zr.at[d], at_z(zd)))
        value = total(z)
        for d, copy in enumerate(arriving):
            copy.wait_recv()
            value = [value[c] + zr[d + 1, c].astype(f32) for c in range(2)]
        return value

    def forward(yd, G, first):
        def block(q, _):
            r = pl.ds(pl.multiple_of(q * 256, 256), 256)
            v = None
            for zd in range(nz):
                g = jnp.concatenate([G[yd, 0, zd], G[yd, 1, zd]], axis=1)
                t = nt_dot(g, T[yd * nz + zd, r, :])
                v = t if v is None else v + t
            for h in range(2):
                part = v[:, 128 * h:128 * h + 128]
                acc[2 * q + h] = part if first else acc[2 * q + h] + part
            return 0

        lax.fori_loop(0, rows // 256, block, 0)

    def gather_forward(tag, value):
        G = s["G" + tag]
        for c in range(2):
            G[y, c, z] = value[c].astype(bf16)
        arriving = []
        for d in range(1, nz):
            arriving.append(push(G.at[y, :, z], G.at[y, :, z], at_z((z + d) % nz)))
        for copy in arriving:
            copy.wait_recv()
        g1 = push(G.at[y], G.at[y], at_y(p1))
        g2 = push(G.at[y], G.at[y], at_y(p2))
        forward(y, G, True)
        g1.wait_recv()
        g2.wait_recv()
        h1 = push(G.at[p2, 0], G.at[p2, 0], at_y(p1))
        h2 = push(G.at[p1, 1], G.at[p1, 1], at_y(p2))
        forward(p1, G, False)
        forward(p2, G, False)
        h1.wait_recv()
        h2.wait_recv()
        forward(far, G, False)
        up, ur = s["up" + tag], s["ur" + tag]
        arriving = []
        for d in range(1, nf):
            to = (me + d) % nf
            up[d] = acc[to].astype(up.dtype)
            arriving.append(push(up.at[d], ur.at[d], at_f(to)))
        total = acc[me]
        for d, copy in enumerate(arriving):
            copy.wait_recv()
            total = total + ur[d + 1].astype(f32)
        slot = me * 128 + lax.broadcasted_iota(jnp.int32, (64, 128), 1)
        return jnp.where(slot < count, total, 0.0)

    def pack(tag, columns):
        at = lax.broadcasted_iota(jnp.int32, (64, 128), 1)
        tile = jnp.zeros((64, 128), f32)
        for k, v in enumerate(columns):
            tile = jnp.where(at == k, v, tile)
        s["sc" + tag][0, :, 0:64] = tile.T[0:8, :]

    def dots(pairs):
        return sum(jnp.sum(a * b, axis=1, keepdims=True) for a, b in pairs)

    def scalar_stage(tag, stage, targets):
        n = len(targets)
        sc, sr = s["sc" + tag], s["sr%d" % stage + tag]
        copies = [push(sc.at[stage], sr.at[i], peer) for i, peer in enumerate(targets)]

        def finish():
            v = sc[stage]
            for i, copy in enumerate(copies):
                copy.wait_recv()
                v = v + sr[i]
            sc[stage + 1] = v

        return finish

    to_f = [at_f((me + d) % nf) for d in range(1, nf)]
    to_y = [at_y((y + d) % NY) for d in range(1, NY)]
    to_z = [at_z((z + d) % nz) for d in range(1, nz)]

    def unpack(tag, n):
        v = s["sc" + tag][3]
        v = jnp.concatenate([v] * 16, axis=0).T
        return [v[0:64, k:k + 1] for k in range(n)]

    s["sca"][0] = jnp.zeros((8, 128), f32)
    s["scb"][0] = jnp.zeros((8, 128), f32)

    b = back_reduce("b", s["yb"], True)
    for c in range(2):
        s["bf"][c] = b[c]
    u = gather_forward("b", b)
    s["uf"][...] = u
    s["ui"][me] = u.astype(bf16)
    arriving = [push(s["ui"].at[me], s["ui"].at[me], peer) for peer in to_f]
    b = [s["bf"][c] for c in range(2)]
    pack("a", [dots([(b[0], b[0]), (b[1], b[1])]), dots([(u, u)])])
    finish = scalar_stage("a", 0, to_f)
    for copy in arriving:
        copy.wait_recv()
    for k in range(nf):
        s["yb"][:, 128 * k:128 * k + 128] = s["ui"][k]
    finish()
    finish = scalar_stage("a", 1, to_y)
    while started:
        started.pop(0).wait_send()
    g = back_reduce("g", s["yb"], False)
    finish()
    finish = scalar_stage("a", 2, to_z)
    finish()
    rr, uu = unpack("a", 2)
    alpha0 = rr / (uu + RIDGE * rr)
    b = [s["bf"][c] for c in range(2)]
    r = [(1.0 - RIDGE * alpha0) * b[c] - alpha0 * g[c] for c in range(2)]
    for c in range(2):
        s["rf"][c] = r[c]
    v = gather_forward("g", r)
    u = s["uf"][...]
    b = [s["bf"][c] for c in range(2)]
    r = [s["rf"][c] for c in range(2)]
    pack("b", [dots([(r[0], r[0]), (r[1], r[1])]), dots([(r[0], b[0]), (r[1], b[1])]),
               dots([(v, v)]), dots([(v, u)])])
    scalar_stage("b", 0, to_f)()
    scalar_stage("b", 1, to_y)()
    scalar_stage("b", 2, to_z)()
    fresh, rb, vv, vu = unpack("b", 4)
    rr, uu = unpack("a", 2)
    alpha0 = rr / (uu + RIDGE * rr)
    beta = fresh / rr
    image = vv + 2.0 * beta * vu + beta * beta * uu
    length = fresh + 2.0 * beta * rb + beta * beta * rr
    alpha1 = fresh / (image + RIDGE * length)
    on_b = jnp.broadcast_to(alpha0 + alpha1 * beta, (64, 128))
    on_r = jnp.broadcast_to(alpha1, (64, 128))

    def finish_chunk(k, _):
        at = pl.ds(pl.multiple_of(k * 128, 128), 128)
        for c in range(2):
            out_ref[c, :, at] = (on_b * s["Gb"][k // nz, c, k % nz].astype(f32)
                                 + on_r * s["Gg"][k // nz, c, k % nz].astype(f32))
        return 0

    lax.fori_loop(0, NY * nz, finish_chunk, 0)
    for copy in started:
        copy.wait_send()


def per_device(nz, nf, inputs, freqs, targets, counts):
    rows, pairs = inputs.shape[0], freqs.shape[1]
    f32, bf16 = jnp.float32, jnp.bfloat16
    copies = 2 * (6 + 2 * (nz - 1) + 4 + (nf - 1)) + (nf - 1) + 2 * (nf - 1 + NY - 1 + nz - 1)
    vmem = pltpu.VMEM
    scratch = {
        "T": vmem((NY * nz, rows, 256), bf16),
        "ph": vmem((rows, 256), f32),
        "acc": vmem((nf, 64, 128), f32),
        "yb": vmem((64, rows), bf16),
        "own": vmem((2, NY, nz, 64, 128), f32),
        "low": vmem((2, NY, nz, 64, 128), bf16),
        "bf": vmem((2, 64, 128), f32),
        "rf": vmem((2, 64, 128), f32),
        "uf": vmem((64, 128), f32),
        "ui": vmem((nf, 64, 128), bf16),
        "send": pltpu.SemaphoreType.DMA((copies,)),
        "recv": pltpu.SemaphoreType.DMA((copies,)),
    }
    for tag, kind in (("b", f32), ("g", bf16)):
        scratch["r1" + tag] = vmem((2, 2, nz, 64, 128), kind)
        scratch["r2" + tag] = vmem((2, nz, 64, 128), kind)
        scratch["st" + tag] = vmem((2, nz, 64, 128), kind)
        scratch["tot" + tag] = vmem((nz, 2, 64, 128), kind)
        scratch["zr" + tag] = vmem((nz, 2, 64, 128), kind)
        scratch["G" + tag] = vmem((NY, 2, nz, 64, 128), bf16)
        scratch["up" + tag] = vmem((nf, 64, 128), bf16)
        scratch["ur" + tag] = vmem((nf, 64, 128), bf16)
    for tag in ("a", "b"):
        scratch["sc" + tag] = vmem((4, 8, 128), f32)
        for stage, n in enumerate((nf, NY, nz)):
            scratch["sr%d" % stage + tag] = vmem((n, 8, 128), f32)
    whole = pl.BlockSpec(memory_space=pltpu.VMEM)
    out = pl.pallas_call(
        functools.partial(kernel, nz, nf, float(pairs * nf) ** -0.5),
        out_shape=jax.ShapeDtypeStruct((2, 64, pairs), f32),
        in_specs=[pl.BlockSpec(memory_space=pltpu.SMEM), whole, whole, whole],
        out_specs=whole,
        scratch_shapes=[scratch],
        compiler_params=pltpu.CompilerParams(
            collective_id=0, has_side_effects=True, vmem_limit_bytes=56 * 2 ** 20),
        cost_estimate=pl.CostEstimate(
            flops=12 * rows * pairs * 64, bytes_accessed=4 * 2 ** 20, transcendentals=0),
    )(counts, inputs, freqs, targets.T)
    return jnp.swapaxes(out, 1, 2)


def solution(mesh):
    nz, nf = mesh.shape["dp"] // NY, mesh.shape["freq"]
    return jax.shard_map(
        functools.partial(per_device, nz, nf),
        mesh=mesh,
        in_specs=(P("dp", None), P(None, "freq"), P("dp", None), P("dp")),
        out_specs=P(None, "freq", None),
        check_vma=False,
    )
```

```python
import functools
import math

import jax
import jax.numpy as jnp
from jax import lax
from jax.experimental import pallas as pl
from jax.experimental.pallas import tpu as pltpu
from jax.sharding import PartitionSpec as P

MESH = pl.DeviceIdType.MESH
RIDGE = 0.5
NY = 4
ROWT = 64

SIN_HALF = (3.14158198, -5.1671413, 2.54188707, -0.554608852)
COS_HALF = (0.999999953, -4.93479283, 4.05841135, -1.33187657, 0.219689611)
INV_TURN = 0.15915494309189535


def nt_dot(a, b):
    return lax.dot_general(a, b, (((1,), (1,)), ((), ())), preferred_element_type=jnp.float32)


def cos_sin(phase, scale):
    gain = math.sqrt(2.0 * scale)
    turns = phase * INV_TURN
    frac = turns - jnp.round(turns)
    sq = frac * frac
    s = SIN_HALF[3] * gain
    for i in (2, 1, 0):
        s = s * sq + SIN_HALF[i] * gain
    c = COS_HALF[4] * gain
    for i in (3, 2, 1, 0):
        c = c * sq + COS_HALF[i] * gain
    s = s * frac
    return scale - s * s, s * c


def kernel(nz, nf, scale, count_ref, x_ref, w_ref, y_ref, out_ref, s):
    rows, half = 128 * nf, nz // 2
    rt, rb = rows // 2, min(256, rows)
    f32, bf16 = jnp.float32, jnp.bfloat16
    dp, me = lax.axis_index("dp"), lax.axis_index("freq")
    z, y = dp // NY, dp % NY
    count = count_ref[0]
    T, acc = s["T"], s["acc"]

    def at_y(v):
        return (z * NY + v, me)

    def at_z(v):
        return (v * NY + y, me)

    def at_f(v):
        return (dp, v)

    to_f = [at_f((me + d) % nf) for d in range(1, nf)]
    to_y = [at_y((y + d) % NY) for d in range(1, NY)]
    to_z = [at_z((z + d) % nz) for d in range(1, nz)]
    far_first = sorted(range(1, nz), key=lambda d: -min(d, nz - d))

    barrier = pltpu.get_barrier_semaphore()
    peers = to_f + to_y + to_z
    for peer in peers:
        pl.semaphore_signal(barrier, inc=1, device_id=peer, device_id_type=MESH)

    pending = []
    used = [0]

    def take(n):
        used[0] += n
        return used[0] - n

    def remote(src, dst, peer, k):
        return pltpu.make_async_remote_copy(
            src_ref=src, dst_ref=dst, send_sem=s["send"].at[k], recv_sem=s["recv"].at[k],
            device_id=peer, device_id_type=MESH)

    def push(src, dst, peer):
        copy = remote(src, dst, peer, take(1))
        copy.start()
        pending.append(copy)
        return copy

    lane = lax.broadcasted_iota(jnp.int32, (64, rows), 1)
    s["yb"][...] = jnp.where(lane < count, y_ref[...].astype(f32), 0.0).astype(bf16)

    def chunks(k, j):
        yd = (y + 1 + j) % NY
        return yd * nz + (z + half + k) % nz, yd * nz + (z + half - 1 - k + nz) % nz

    def back_reducer(tag):
        out, own, r1, tot, zr = (s[k + tag] for k in ("out", "own", "r1", "tot", "zr"))
        base_y, base_z = take(half * (NY - 1)), take(nz)

        def store(k, j, h, v, more):
            for c in range(2):
                part = v[:, 128 * c:128 * c + 128]
                ref = out.at[j, k, h, c] if j < NY - 1 else own.at[k, h, c]
                if more:
                    part = part + ref[...].astype(f32)
                ref[...] = part.astype(ref.dtype)

        def y_copy(k, j):
            return remote(out.at[j, k], r1.at[j, k], to_y[j], base_y + k * (NY - 1) + j)

        def z_copy(d):
            return remote(tot.at[d], zr.at[d], at_z((z + d) % nz), base_z + d)

        def sum_y(k, h):
            v = [own[k, h, c] for c in range(2)]
            for j in range(NY - 1):
                v = [v[c] + r1[j, k, h, c].astype(f32) for c in range(2)]
            return v

        def send_z(k, h, d):
            for c, v in enumerate(sum_y(k, h)):
                tot[d, c] = v.astype(tot.dtype)
            z_copy(d).start()

        def wait_y(k):
            for j in range(NY - 1):
                y_copy(k, j).wait_recv()

        def send_batch(k):
            wait_y(k)
            send_z(k, 0, half + k)
            send_z(k, 1, half - 1 - k)

        def last():
            wait_y(half - 1)
            send_z(half - 1, 0, nz - 1)
            value = sum_y(half - 1, 1)
            for d in range(1, nz):
                z_copy(d).wait_recv()
                value = [value[c] + zr[d, c].astype(f32) for c in range(2)]
            for k in range(half):
                for j in range(NY - 1):
                    pending.append(y_copy(k, j))
            for d in range(1, nz):
                pending.append(z_copy(d))
            return value

        return store, y_copy, send_batch, last

    def features_back(tag):
        store, y_copy, send_batch, last = back_reducer(tag)
        phases = (s["ph0"], s["ph1"])

        def phase(k, j, i):
            w = [w_ref[:, pl.ds(pl.multiple_of(c * 128, 128), 128)] for c in chunks(k, j)]
            return jnp.dot(x_ref[rt * i:rt * i + rt, :], jnp.concatenate(w, axis=1),
                           preferred_element_type=f32)

        def back(k, j, i):
            for h, chunk in enumerate(chunks(k, j)):
                v = jnp.dot(s["yb"][:, rt * i:rt * i + rt], T[chunk, rt * i:rt * i + rt, :],
                            preferred_element_type=f32)
                store(k, j, h, v, i > 0)

        for chunk in chunks(0, NY - 1):
            T[chunk] = jnp.zeros((rows, 256), bf16)
        phases[0][...] = phase(0, 0, 0)

        def batch(k, _):
            for j in range(NY):
                pk, pj = (k, j - 1) if j else (jnp.maximum(k - 1, 0), NY - 1)
                nk, nj = (k, j + 1) if j < NY - 1 else ((k + 1) % half, 0)
                here = chunks(k, j)
                for i in range(2):
                    back(pk, pj, i)
                    phases[1 - i][...] = phase(k, j, 1) if i == 0 else phase(nk, nj, 0)
                    for r in range(0, rt, ROWT):
                        c, v = cos_sin(phases[i][r:r + ROWT, :], scale)
                        c, v = c.astype(bf16), v.astype(bf16)
                        for h in range(2):
                            at = pl.ds(rt * i + r, ROWT)
                            T[here[h], at, 0:128] = c[:, 128 * h:128 * h + 128]
                            T[here[h], at, 128:256] = v[:, 128 * h:128 * h + 128]
                if j == 1:
                    @pl.when(k == 0)
                    def _():
                        pl.semaphore_wait(barrier, len(peers))
                if j:
                    y_copy(k, j - 1).start()
            pl.when(k > 0)(lambda: send_batch(k - 1))
            return 0

        lax.fori_loop(0, half, batch, 0)
        for i in range(2):
            back(half - 1, NY - 1, i)
        return last()

    def only_back(tag, rhs, between):
        store, y_copy, send_batch, last = back_reducer(tag)

        def batch(k, _):
            for j in range(NY):
                for h, chunk in enumerate(chunks(k, j)):
                    store(k, j, h, jnp.dot(rhs[...], T[chunk], preferred_element_type=f32), False)
                if j < NY - 1:
                    y_copy(k, j).start()
            return 0

        lax.fori_loop(0, half, batch, 0)
        between()

        def sums(k, _):
            send_batch(k)
            return 0

        lax.fori_loop(0, half - 1, sums, 0)
        return last()

    def forward(G, which, first=False):
        def block(q, _):
            r = pl.ds(pl.multiple_of(q * rb, rb), rb)
            v = None
            for yd, zd in which:
                g = jnp.concatenate([G[yd, zd, 0], G[yd, zd, 1]], axis=1)
                t = nt_dot(g, T[yd * nz + zd, r, :])
                v = t if v is None else v + t
            for h in range(rb // 128):
                part = v[:, 128 * h:128 * h + 128]
                at = q * (rb // 128) + h
                acc[at] = part if first else acc[at] + part
            return 0

        lax.fori_loop(0, rows // rb, block, 0)

    def gather_forward(tag, value):
        G = s["G" + tag]
        for c in range(2):
            G[y, z, c] = value[c].astype(bf16)
        landing = [push(G.at[y, z], G.at[y, z], to_z[d - 1]) for d in far_first]
        across = [[push(G.at[y, z], G.at[y, z], peer) for peer in to_y]]
        forward(G, [(y, z)], True)
        for copy, d in zip(landing, far_first):
            zd = (z - d + nz) % nz
            copy.wait_recv()
            across.append([push(G.at[y, zd], G.at[y, zd], peer) for peer in to_y])
            forward(G, [(y, zd)])
        for copies, d in zip(across, [0] + far_first):
            for copy in copies:
                copy.wait_recv()
            forward(G, [((y - j + NY) % NY, (z - d + nz) % nz) for j in range(1, NY)])
        up, ur = s["up" + tag], s["ur" + tag]
        arriving = []
        for d in range(1, nf):
            to = (me + d) % nf
            up[d] = acc[to].astype(up.dtype)
            arriving.append(push(up.at[d], ur.at[d], at_f(to)))
        total = acc[me]
        for d, copy in enumerate(arriving):
            copy.wait_recv()
            total = total + ur[d + 1].astype(f32)
        slot = me * 128 + lax.broadcasted_iota(jnp.int32, (64, 128), 1)
        return jnp.where(slot < count, total, 0.0)

    def pack(tag, columns):
        at = lax.broadcasted_iota(jnp.int32, (64, 128), 1)
        tile = jnp.zeros((64, 128), f32)
        for k, v in enumerate(columns):
            tile = jnp.where(at == k, v, tile)
        s["sc" + tag][0, :, 0:64] = tile.T[0:8, :]

    def dots(pairs):
        return sum(jnp.sum(a * b, axis=1, keepdims=True) for a, b in pairs)

    def scalar_stage(tag, stage, targets):
        sc, sr = s["sc" + tag], s["sr%d" % stage + tag]
        copies = [push(sc.at[stage], sr.at[i], peer) for i, peer in enumerate(targets)]

        def finish():
            v = sc[stage]
            for i, copy in enumerate(copies):
                copy.wait_recv()
                v = v + sr[i]
            sc[stage + 1] = v

        return finish

    def unpack(tag, n):
        v = s["sc" + tag][3]
        v = jnp.concatenate([v] * 16, axis=0).T
        return [v[0:64, k:k + 1] for k in range(n)]

    s["sca"][0] = jnp.zeros((8, 128), f32)
    s["scb"][0] = jnp.zeros((8, 128), f32)

    b = features_back("b")
    for c in range(2):
        s["bf"][c] = b[c]
    u = gather_forward("b", b)
    s["uf"][...] = u
    s["ui"][me] = u.astype(bf16)
    arriving = [push(s["ui"].at[me], s["ui"].at[me], peer) for peer in to_f]
    b = [s["bf"][c] for c in range(2)]
    pack("a", [dots([(b[0], b[0]), (b[1], b[1])]), dots([(u, u)])])
    finish = scalar_stage("a", 0, to_f)
    for copy in arriving:
        copy.wait_recv()
    for k in range(nf):
        s["yb"][:, 128 * k:128 * k + 128] = s["ui"][k]
    finish()
    finish = scalar_stage("a", 1, to_y)
    ends = []

    def between():
        finish()
        ends.append(scalar_stage("a", 2, to_z))

    g = only_back("g", s["yb"], between)
    ends[0]()
    rr, uu = unpack("a", 2)
    alpha0 = rr / (uu + RIDGE * rr)
    b = [s["bf"][c] for c in range(2)]
    r = [(1.0 - RIDGE * alpha0) * b[c] - alpha0 * g[c] for c in range(2)]
    for c in range(2):
        s["rf"][c] = r[c]
    v = gather_forward("g", r)
    u = s["uf"][...]
    b = [s["bf"][c] for c in range(2)]
    r = [s["rf"][c] for c in range(2)]
    pack("b", [dots([(r[0], r[0]), (r[1], r[1])]), dots([(r[0], b[0]), (r[1], b[1])]),
               dots([(v, v)]), dots([(v, u)])])
    scalar_stage("b", 0, to_f)()
    scalar_stage("b", 1, to_y)()
    scalar_stage("b", 2, to_z)()
    fresh, rb_, vv, vu = unpack("b", 4)
    rr, uu = unpack("a", 2)
    alpha0 = rr / (uu + RIDGE * rr)
    beta = fresh / rr
    image = vv + 2.0 * beta * vu + beta * beta * uu
    length = fresh + 2.0 * beta * rb_ + beta * beta * rr
    alpha1 = fresh / (image + RIDGE * length)
    on_b = jnp.broadcast_to(alpha0 + alpha1 * beta, (64, 128))
    on_r = jnp.broadcast_to(alpha1, (64, 128))

    def finish_chunk(k, _):
        at = pl.ds(pl.multiple_of(k * 128, 128), 128)
        for c in range(2):
            out_ref[c, :, at] = (on_b * s["Gb"][k // nz, k % nz, c].astype(f32)
                                 + on_r * s["Gg"][k // nz, k % nz, c].astype(f32))
        return 0

    lax.fori_loop(0, NY * nz, finish_chunk, 0)
    for copy in pending:
        copy.wait_send()


def per_device(nz, nf, inputs, freqs, targets, counts):
    rows, pairs = inputs.shape[0], freqs.shape[1]
    f32, bf16 = jnp.float32, jnp.bfloat16
    half = nz // 2
    copies = 2 * (half * (NY - 1) + nz + nz - 1 + nz * (NY - 1) + nf - 1) + nf - 1 + 2 * (nf + NY + nz - 3)
    vmem = pltpu.VMEM
    scratch = {
        "T": vmem((NY * nz, rows, 256), bf16),
        "ph0": vmem((rows // 2, 256), f32),
        "ph1": vmem((rows // 2, 256), f32),
        "acc": vmem((nf, 64, 128), f32),
        "yb": vmem((64, rows), bf16),
        "bf": vmem((2, 64, 128), f32),
        "rf": vmem((2, 64, 128), f32),
        "uf": vmem((64, 128), f32),
        "ui": vmem((nf, 64, 128), bf16),
        "send": pltpu.SemaphoreType.DMA((copies,)),
        "recv": pltpu.SemaphoreType.DMA((copies,)),
    }
    for tag, kind in (("b", f32), ("g", bf16)):
        scratch["out" + tag] = vmem((NY - 1, half, 2, 2, 64, 128), kind)
        scratch["own" + tag] = vmem((half, 2, 2, 64, 128), f32)
        scratch["r1" + tag] = vmem((NY - 1, half, 2, 2, 64, 128), kind)
        scratch["tot" + tag] = vmem((nz, 2, 64, 128), kind)
        scratch["zr" + tag] = vmem((nz, 2, 64, 128), kind)
        scratch["G" + tag] = vmem((NY, nz, 2, 64, 128), bf16)
        scratch["up" + tag] = vmem((nf, 64, 128), bf16)
        scratch["ur" + tag] = vmem((nf, 64, 128), bf16)
    for tag in ("a", "b"):
        scratch["sc" + tag] = vmem((4, 8, 128), f32)
        for stage, n in enumerate((nf, NY, nz)):
            scratch["sr%d" % stage + tag] = vmem((n, 8, 128), f32)
    whole = pl.BlockSpec(memory_space=pltpu.VMEM)
    out = pl.pallas_call(
        functools.partial(kernel, nz, nf, float(pairs * nf) ** -0.5),
        out_shape=jax.ShapeDtypeStruct((2, 64, pairs), f32),
        in_specs=[pl.BlockSpec(memory_space=pltpu.SMEM), whole, whole, whole],
        out_specs=whole,
        scratch_shapes=[scratch],
        compiler_params=pltpu.CompilerParams(
            collective_id=0, has_side_effects=True, vmem_limit_bytes=56 * 2 ** 20),
        cost_estimate=pl.CostEstimate(
            flops=12 * rows * pairs * 64, bytes_accessed=4 * 2 ** 20, transcendentals=0),
    )(counts, inputs, freqs, targets.T)
    return jnp.swapaxes(out, 1, 2)


def solution(mesh):
    nz, nf = mesh.shape["dp"] // NY, mesh.shape["freq"]
    return jax.shard_map(
        functools.partial(per_device, nz, nf),
        mesh=mesh,
        in_specs=(P("dp", None), P(None, "freq"), P("dp", None), P("dp")),
        out_specs=P(None, "freq", None),
        check_vma=False,
    )
```

```python
import functools
import math

import jax
import jax.numpy as jnp
from jax import lax
from jax.experimental import pallas as pl
from jax.experimental.pallas import tpu as pltpu
from jax.sharding import PartitionSpec as P

MESH = pl.DeviceIdType.MESH
RIDGE = 0.5
NY = 4
ROWT = 64
STAGES = {"a": ("f", "y", "z"), "b": ("yf", "z")}

SIN_HALF = (3.14158198, -5.1671413, 2.54188707, -0.554608852)
COS_HALF = (0.999999953, -4.93479283, 4.05841135, -1.33187657, 0.219689611)
INV_TURN = 0.15915494309189535


def nt_dot(a, b):
    return lax.dot_general(a, b, (((1,), (1,)), ((), ())), preferred_element_type=jnp.float32)


def cos_sin(phase, scale):
    gain = math.sqrt(2.0 * scale)
    turns = phase * INV_TURN
    frac = turns - jnp.round(turns)
    sq = frac * frac
    s = SIN_HALF[3] * gain
    for i in (2, 1, 0):
        s = s * sq + SIN_HALF[i] * gain
    c = COS_HALF[4] * gain
    for i in (3, 2, 1, 0):
        c = c * sq + COS_HALF[i] * gain
    s = s * frac
    return scale - s * s, s * c


def kernel(nz, nf, scale, count_ref, x_ref, w_ref, y_ref, out_ref, s):
    rows, half = 128 * nf, nz // 2
    rt = rows // 2
    f32, bf16 = jnp.float32, jnp.bfloat16
    dp, me = lax.axis_index("dp"), lax.axis_index("freq")
    z, y = dp // NY, dp % NY
    count = count_ref[0]
    T, acc = s["T"], s["acc"]

    def at_y(v):
        return (z * NY + v, me)

    def at_z(v):
        return (v * NY + y, me)

    def at_f(v):
        return (dp, v)

    to_f = [at_f((me + d) % nf) for d in range(1, nf)]
    to_y = [at_y((y + d) % NY) for d in range(1, NY)]
    to_z = [at_z((z + d) % nz) for d in range(1, nz)]
    to_yf = [(z * NY + (y + j) % NY, (me + d) % nf) for j in range(NY) for d in range(nf) if j + d]
    far_first = sorted(range(1, nz), key=lambda d: -min(d, nz - d))

    barrier = pltpu.get_barrier_semaphore()
    peers = to_yf + to_z
    for peer in peers:
        pl.semaphore_signal(barrier, inc=1, device_id=peer, device_id_type=MESH)

    pending = []
    used = [0]

    def take(n):
        used[0] += n
        return used[0] - n

    def remote(src, dst, peer, k):
        return pltpu.make_async_remote_copy(
            src_ref=src, dst_ref=dst, send_sem=s["send"].at[k], recv_sem=s["recv"].at[k],
            device_id=peer, device_id_type=MESH)

    def push(src, dst, peer):
        copy = remote(src, dst, peer, take(1))
        copy.start()
        pending.append(copy)
        return copy

    lane = lax.broadcasted_iota(jnp.int32, (64, rows), 1)
    s["yb"][...] = jnp.where(lane < count, y_ref[...].astype(f32), 0.0).astype(bf16)

    def chunks(k, j):
        yd = (y + 1 + j) % NY
        return yd * nz + (z + half + k) % nz, yd * nz + (z + half - 1 - k + nz) % nz

    def back_reducer(tag):
        out, own, r1, tot, zr = (s[k + tag] for k in ("out", "own", "r1", "tot", "zr"))
        base_y, base_z = take(half * (NY - 1)), take(nz)

        def store(k, j, h, v, more):
            for c in range(2):
                part = v[:, 128 * c:128 * c + 128]
                ref = out.at[j, k, h, c] if j < NY - 1 else own.at[k, h, c]
                if more:
                    part = part + ref[...].astype(f32)
                ref[...] = part.astype(ref.dtype)

        def y_copy(k, j):
            return remote(out.at[j, k], r1.at[j, k], to_y[j], base_y + k * (NY - 1) + j)

        def z_copy(d):
            return remote(tot.at[d], zr.at[d], at_z((z + d) % nz), base_z + d)

        def sum_y(k, h):
            v = [own[k, h, c] for c in range(2)]
            for j in range(NY - 1):
                v = [v[c] + r1[j, k, h, c].astype(f32) for c in range(2)]
            return v

        def send_z(k, h, d):
            for c, v in enumerate(sum_y(k, h)):
                tot[d, c] = v.astype(tot.dtype)
            z_copy(d).start()

        def wait_y(k):
            for j in range(NY - 1):
                y_copy(k, j).wait_recv()

        def send_batch(k):
            wait_y(k)
            send_z(k, 0, half + k)
            send_z(k, 1, half - 1 - k)

        def last():
            wait_y(half - 1)
            send_z(half - 1, 0, nz - 1)
            value = sum_y(half - 1, 1)
            for d in range(1, nz):
                z_copy(d).wait_recv()
                value = [value[c] + zr[d, c].astype(f32) for c in range(2)]
            for k in range(half):
                for j in range(NY - 1):
                    pending.append(y_copy(k, j))
            for d in range(1, nz):
                pending.append(z_copy(d))
            return value

        return store, y_copy, send_batch, last

    def features_back(tag):
        store, y_copy, send_batch, last = back_reducer(tag)
        phases = (s["ph0"], s["ph1"])

        def phase(k, j, i):
            w = [w_ref[:, pl.ds(pl.multiple_of(c * 128, 128), 128)] for c in chunks(k, j)]
            return jnp.dot(x_ref[rt * i:rt * i + rt, :], jnp.concatenate(w, axis=1),
                           preferred_element_type=f32)

        def back(k, j, i):
            for h, chunk in enumerate(chunks(k, j)):
                v = jnp.dot(s["yb"][:, rt * i:rt * i + rt], T[chunk, rt * i:rt * i + rt, :],
                            preferred_element_type=f32)
                store(k, j, h, v, i > 0)

        for chunk in chunks(0, NY - 1):
            T[chunk] = jnp.zeros((rows, 256), bf16)
        phases[0][...] = phase(0, 0, 0)

        def batch(k, _):
            for j in range(NY):
                pk, pj = (k, j - 1) if j else (jnp.maximum(k - 1, 0), NY - 1)
                nk, nj = (k, j + 1) if j < NY - 1 else ((k + 1) % half, 0)
                here = chunks(k, j)
                for i in range(2):
                    back(pk, pj, i)
                    phases[1 - i][...] = phase(k, j, 1) if i == 0 else phase(nk, nj, 0)
                    for r in range(0, rt, ROWT):
                        c, v = cos_sin(phases[i][r:r + ROWT, :], scale)
                        c, v = c.astype(bf16), v.astype(bf16)
                        for h in range(2):
                            at = pl.ds(rt * i + r, ROWT)
                            T[here[h], at, 0:128] = c[:, 128 * h:128 * h + 128]
                            T[here[h], at, 128:256] = v[:, 128 * h:128 * h + 128]
                if j == 1:
                    @pl.when(k == 0)
                    def _():
                        pl.semaphore_wait(barrier, len(peers))
                if j:
                    y_copy(k, j - 1).start()
            pl.when(k > 0)(lambda: send_batch(k - 1))
            return 0

        lax.fori_loop(0, half, batch, 0)
        for i in range(2):
            back(half - 1, NY - 1, i)
        return last()

    def only_back(tag, rhs, between):
        store, y_copy, send_batch, last = back_reducer(tag)

        def batch(k, _):
            for j in range(NY):
                for h, chunk in enumerate(chunks(k, j)):
                    store(k, j, h, jnp.dot(rhs[...], T[chunk], preferred_element_type=f32), False)
                if j < NY - 1:
                    y_copy(k, j).start()
            return 0

        lax.fori_loop(0, half, batch, 0)
        between()

        def sums(k, _):
            send_batch(k)
            return 0

        lax.fori_loop(0, half - 1, sums, 0)
        return last()

    def forward(G, which, first=False):
        v = None
        for yd, zd in which:
            g = jnp.concatenate([G[yd, zd, 0], G[yd, zd, 1]], axis=1)
            t = nt_dot(T[yd * nz + zd], g)
            v = t if v is None else v + t
        v = v.T
        for h in range(nf):
            part = v[:, 128 * h:128 * h + 128]
            acc[h] = part if first else acc[h] + part

    def gather_forward(tag, value):
        G = s["G" + tag]
        for c in range(2):
            G[y, z, c] = value[c].astype(bf16)
        landing = [push(G.at[y, z], G.at[y, z], to_z[d - 1]) for d in far_first]
        across = [[push(G.at[y, z], G.at[y, z], peer) for peer in to_y]]
        forward(G, [(y, z)], True)
        for copy, d in zip(landing, far_first):
            zd = (z - d + nz) % nz
            copy.wait_recv()
            across.append([push(G.at[y, zd], G.at[y, zd], peer) for peer in to_y])
            forward(G, [(y, zd)])
        for copies, d in zip(across, [0] + far_first):
            for copy in copies:
                copy.wait_recv()
            forward(G, [((y - j + NY) % NY, (z - d + nz) % nz) for j in range(1, NY)])
        up, ur = s["up" + tag], s["ur" + tag]
        arriving = []
        for d in range(1, nf):
            to = (me + d) % nf
            up[d] = acc[to].astype(up.dtype)
            arriving.append(push(up.at[d], ur.at[d], at_f(to)))
        total = acc[me]
        for d, copy in enumerate(arriving):
            copy.wait_recv()
            total = total + ur[d + 1].astype(f32)
        slot = me * 128 + lax.broadcasted_iota(jnp.int32, (64, 128), 1)
        return jnp.where(slot < count, total, 0.0)

    def pack(tag, columns):
        at = lax.broadcasted_iota(jnp.int32, (64, 128), 1)
        tile = jnp.zeros((64, 128), f32)
        for k, v in enumerate(columns):
            tile = jnp.where(at == k, v, tile)
        s["sc" + tag][0, :, 0:64] = tile.T[0:8, :]

    def dots(pairs):
        return sum(jnp.sum(a * b, axis=1, keepdims=True) for a, b in pairs)

    def scalar_stage(tag, stage, targets):
        sc, sr = s["sc" + tag], s["sr%d" % stage + tag]
        copies = [push(sc.at[stage], sr.at[i], peer) for i, peer in enumerate(targets)]

        def finish():
            v = sc[stage]
            for i, copy in enumerate(copies):
                copy.wait_recv()
                v = v + sr[i]
            sc[stage + 1] = v

        return finish

    def unpack(tag, n):
        v = s["sc" + tag][len(STAGES[tag])]
        v = jnp.concatenate([v] * 16, axis=0).T
        return [v[0:64, k:k + 1] for k in range(n)]

    s["sca"][0] = jnp.zeros((8, 128), f32)
    s["scb"][0] = jnp.zeros((8, 128), f32)

    b = features_back("b")
    for c in range(2):
        s["bf"][c] = b[c]
    u = gather_forward("b", b)
    s["uf"][...] = u
    s["ui"][me] = u.astype(bf16)
    arriving = [push(s["ui"].at[me], s["ui"].at[me], peer) for peer in to_f]
    b = [s["bf"][c] for c in range(2)]
    pack("a", [dots([(b[0], b[0]), (b[1], b[1])]), dots([(u, u)])])
    finish = scalar_stage("a", 0, to_f)
    for copy in arriving:
        copy.wait_recv()
    for k in range(nf):
        s["yb"][:, 128 * k:128 * k + 128] = s["ui"][k]
    finish()
    finish = scalar_stage("a", 1, to_y)
    ends = []

    def between():
        finish()
        ends.append(scalar_stage("a", 2, to_z))

    g = only_back("g", s["yb"], between)
    ends[0]()
    rr, uu = unpack("a", 2)
    alpha0 = rr / (uu + RIDGE * rr)
    b = [s["bf"][c] for c in range(2)]
    r = [(1.0 - RIDGE * alpha0) * b[c] - alpha0 * g[c] for c in range(2)]
    for c in range(2):
        s["rf"][c] = r[c]
    v = gather_forward("g", r)
    u = s["uf"][...]
    b = [s["bf"][c] for c in range(2)]
    r = [s["rf"][c] for c in range(2)]
    pack("b", [dots([(r[0], r[0]), (r[1], r[1])]), dots([(r[0], b[0]), (r[1], b[1])]),
               dots([(v, v)]), dots([(v, u)])])
    scalar_stage("b", 0, to_yf)()
    scalar_stage("b", 1, to_z)()
    fresh, rb_, vv, vu = unpack("b", 4)
    rr, uu = unpack("a", 2)
    alpha0 = rr / (uu + RIDGE * rr)
    beta = fresh / rr
    image = vv + 2.0 * beta * vu + beta * beta * uu
    length = fresh + 2.0 * beta * rb_ + beta * beta * rr
    alpha1 = fresh / (image + RIDGE * length)
    on_b = jnp.broadcast_to(alpha0 + alpha1 * beta, (64, 128))
    on_r = jnp.broadcast_to(alpha1, (64, 128))

    def finish_chunk(k, _):
        at = pl.ds(pl.multiple_of(k * 128, 128), 128)
        for c in range(2):
            out_ref[c, :, at] = (on_b * s["Gb"][k // nz, k % nz, c].astype(f32)
                                 + on_r * s["Gg"][k // nz, k % nz, c].astype(f32))
        return 0

    lax.fori_loop(0, NY * nz, finish_chunk, 0)
    for copy in pending:
        copy.wait_send()


def per_device(nz, nf, inputs, freqs, targets, counts):
    rows, pairs = inputs.shape[0], freqs.shape[1]
    f32, bf16 = jnp.float32, jnp.bfloat16
    half = nz // 2
    copies = 2 * (half * (NY - 1) + nz + nz - 1 + nz * (NY - 1) + nf - 1) + nf - 1 + (nf + NY + nz - 3) + (NY * nf + nz - 2)
    vmem = pltpu.VMEM
    scratch = {
        "T": vmem((NY * nz, rows, 256), bf16),
        "ph0": vmem((rows // 2, 256), f32),
        "ph1": vmem((rows // 2, 256), f32),
        "acc": vmem((nf, 64, 128), f32),
        "yb": vmem((64, rows), bf16),
        "bf": vmem((2, 64, 128), f32),
        "rf": vmem((2, 64, 128), f32),
        "uf": vmem((64, 128), f32),
        "ui": vmem((nf, 64, 128), bf16),
        "send": pltpu.SemaphoreType.DMA((copies,)),
        "recv": pltpu.SemaphoreType.DMA((copies,)),
    }
    for tag, kind in (("b", f32), ("g", bf16)):
        scratch["out" + tag] = vmem((NY - 1, half, 2, 2, 64, 128), kind)
        scratch["own" + tag] = vmem((half, 2, 2, 64, 128), f32)
        scratch["r1" + tag] = vmem((NY - 1, half, 2, 2, 64, 128), kind)
        scratch["tot" + tag] = vmem((nz, 2, 64, 128), kind)
        scratch["zr" + tag] = vmem((nz, 2, 64, 128), kind)
        scratch["G" + tag] = vmem((NY, nz, 2, 64, 128), bf16)
        scratch["up" + tag] = vmem((nf, 64, 128), bf16)
        scratch["ur" + tag] = vmem((nf, 64, 128), bf16)
    size = {"f": nf, "y": NY, "z": nz, "yf": NY * nf}
    for tag, stages in STAGES.items():
        scratch["sc" + tag] = vmem((len(stages) + 1, 8, 128), f32)
        for stage, group in enumerate(stages):
            scratch["sr%d" % stage + tag] = vmem((size[group], 8, 128), f32)
    whole = pl.BlockSpec(memory_space=pltpu.VMEM)
    out = pl.pallas_call(
        functools.partial(kernel, nz, nf, float(pairs * nf) ** -0.5),
        out_shape=jax.ShapeDtypeStruct((2, 64, pairs), f32),
        in_specs=[pl.BlockSpec(memory_space=pltpu.SMEM), whole, whole, whole],
        out_specs=whole,
        scratch_shapes=[scratch],
        compiler_params=pltpu.CompilerParams(
            collective_id=0, has_side_effects=True, vmem_limit_bytes=56 * 2 ** 20),
        cost_estimate=pl.CostEstimate(
            flops=12 * rows * pairs * 64, bytes_accessed=4 * 2 ** 20, transcendentals=0),
    )(counts, inputs, freqs, targets.T)
    return jnp.swapaxes(out, 1, 2)


def solution(mesh):
    nz, nf = mesh.shape["dp"] // NY, mesh.shape["freq"]
    return jax.shard_map(
        functools.partial(per_device, nz, nf),
        mesh=mesh,
        in_specs=(P("dp", None), P(None, "freq"), P("dp", None), P("dp")),
        out_specs=P(None, "freq", None),
        check_vma=False,
    )
```

```python
import functools
import math

import jax
import jax.numpy as jnp
from jax import lax
from jax.experimental import pallas as pl
from jax.experimental.pallas import tpu as pltpu
from jax.sharding import PartitionSpec as P

MESH = pl.DeviceIdType.MESH
RIDGE = 0.5
NY = 4
ROWT = 64
STAGES = {"a": ("f", "y", "z"), "b": ("yf", "z")}

SIN_HALF = (3.14158198, -5.1671413, 2.54188707, -0.554608852)
COS_HALF = (0.999999953, -4.93479283, 4.05841135, -1.33187657, 0.219689611)
INV_TURN = 0.15915494309189535


def nt_dot(a, b):
    return lax.dot_general(a, b, (((1,), (1,)), ((), ())), preferred_element_type=jnp.float32)


def cos_sin(phase, scale):
    gain = math.sqrt(2.0 * scale)
    turns = phase * INV_TURN
    frac = turns - jnp.round(turns)
    sq = frac * frac
    s = SIN_HALF[3] * gain
    for i in (2, 1, 0):
        s = s * sq + SIN_HALF[i] * gain
    c = COS_HALF[4] * gain
    for i in (3, 2, 1, 0):
        c = c * sq + COS_HALF[i] * gain
    s = s * frac
    return scale - s * s, s * c


def kernel(nz, nf, scale, count_ref, x_ref, w_ref, y_ref, out_ref, s):
    rows, half = 128 * nf, nz // 2
    rt = rows // 2
    f32, bf16 = jnp.float32, jnp.bfloat16
    dp, me = lax.axis_index("dp"), lax.axis_index("freq")
    z, y = dp // NY, dp % NY
    count = count_ref[0]
    T, acc = s["T"], s["acc"]

    def at_y(v):
        return (z * NY + v, me)

    def at_z(v):
        return (v * NY + y, me)

    def at_f(v):
        return (dp, v)

    to_f = [at_f((me + d) % nf) for d in range(1, nf)]
    to_y = [at_y((y + d) % NY) for d in range(1, NY)]
    to_z = [at_z((z + d) % nz) for d in range(1, nz)]
    to_yf = [(z * NY + (y + j) % NY, (me + d) % nf) for j in range(NY) for d in range(nf) if j + d]

    barrier = pltpu.get_barrier_semaphore()
    peers = to_yf + to_z
    for peer in peers:
        pl.semaphore_signal(barrier, inc=1, device_id=peer, device_id_type=MESH)

    pending = []
    used = [0]

    def take(n):
        used[0] += n
        return used[0] - n

    def remote(src, dst, peer, k):
        return pltpu.make_async_remote_copy(
            src_ref=src, dst_ref=dst, send_sem=s["send"].at[k], recv_sem=s["recv"].at[k],
            device_id=peer, device_id_type=MESH)

    def push(src, dst, peer):
        copy = remote(src, dst, peer, take(1))
        copy.start()
        pending.append(copy)
        return copy

    lane = lax.broadcasted_iota(jnp.int32, (64, rows), 1)
    s["yb"][...] = jnp.where(lane < count, y_ref[...].astype(f32), 0.0).astype(bf16)

    def chunks(k, j):
        yd = (y + 1 + j) % NY
        return yd * nz + (z + half + k) % nz, yd * nz + (z + half - 1 - k + nz) % nz

    def back_reducer(tag):
        out, own, r1, tot, zr = (s[k + tag] for k in ("out", "own", "r1", "tot", "zr"))
        base_y, base_z = take(half * (NY - 1)), take(nz)

        def store(k, j, h, v, more=True):
            for c in range(2):
                value = v[:, 128 * c:128 * c + 128]
                if tag == "b":
                    if more:
                        value = value + s["part"][h, c]
                    else:
                        s["part"][h, c] = value
                        continue
                if j == NY - 1:
                    own[k, h, c] = value
                    continue
                high = value.astype(bf16)
                out[j, k, h, c] = high
                if tag == "b":
                    s["lo"][j, k, h, c] = (value - high.astype(f32)).astype(bf16)

        def y_copy(k, j):
            return remote(out.at[j, k], r1.at[j, k], to_y[j], base_y + k * (NY - 1) + j)

        def z_copy(d):
            return remote(tot.at[d], zr.at[d], at_z((z + d) % nz), base_z + d)

        def sum_y(k, h):
            v = [own[k, h, c] for c in range(2)]
            for j in range(NY - 1):
                v = [v[c] + r1[j, k, h, c].astype(f32) for c in range(2)]
            return v

        def send_z(k, h, d):
            for c, v in enumerate(sum_y(k, h)):
                high = v.astype(bf16)
                tot[d, c] = high
                if tag == "b":
                    s["tl"][d, c] = v - high.astype(f32)
            z_copy(d).start()

        def wait_y(k):
            for j in range(NY - 1):
                y_copy(k, j).wait_recv()

        def send_batch(k):
            wait_y(k)
            send_z(k, 0, half + k)
            send_z(k, 1, half - 1 - k)

        def last():
            wait_y(half - 1)
            send_z(half - 1, 0, nz - 1)
            value = sum_y(half - 1, 1)
            for d in range(1, nz):
                z_copy(d).wait_recv()
                value = [value[c] + zr[d, c].astype(f32) for c in range(2)]
            for k in range(half):
                for j in range(NY - 1):
                    pending.append(y_copy(k, j))
            for d in range(1, nz):
                pending.append(z_copy(d))
            return value

        return store, y_copy, send_batch, last

    def features_back(tag):
        store, y_copy, send_batch, last = back_reducer(tag)
        phases = (s["ph0"], s["ph1"])

        def phase(k, j, i):
            w = [w_ref[:, pl.ds(pl.multiple_of(c * 128, 128), 128)] for c in chunks(k, j)]
            return jnp.dot(x_ref[rt * i:rt * i + rt, :], jnp.concatenate(w, axis=1),
                           preferred_element_type=f32)

        def back(k, j, i):
            for h, chunk in enumerate(chunks(k, j)):
                v = jnp.dot(s["yb"][:, rt * i:rt * i + rt], T[chunk, rt * i:rt * i + rt, :],
                            preferred_element_type=f32)
                store(k, j, h, v, i > 0)

        for chunk in chunks(0, NY - 1):
            T[chunk] = jnp.zeros((rows, 256), bf16)
        phases[0][...] = phase(0, 0, 0)

        def batch(k, _):
            for j in range(NY):
                pk, pj = (k, j - 1) if j else (jnp.maximum(k - 1, 0), NY - 1)
                nk, nj = (k, j + 1) if j < NY - 1 else ((k + 1) % half, 0)
                here = chunks(k, j)
                for i in range(2):
                    back(pk, pj, i)
                    phases[1 - i][...] = phase(k, j, 1) if i == 0 else phase(nk, nj, 0)
                    for r in range(0, rt, ROWT):
                        c, v = cos_sin(phases[i][r:r + ROWT, :], scale)
                        c, v = c.astype(bf16), v.astype(bf16)
                        for h in range(2):
                            at = pl.ds(rt * i + r, ROWT)
                            T[here[h], at, 0:128] = c[:, 128 * h:128 * h + 128]
                            T[here[h], at, 128:256] = v[:, 128 * h:128 * h + 128]
                if j == 1:
                    @pl.when(k == 0)
                    def _():
                        pl.semaphore_wait(barrier, len(peers))
                if j:
                    y_copy(k, j - 1).start()
            pl.when(k > 0)(lambda: send_batch(k - 1))
            return 0

        lax.fori_loop(0, half, batch, 0)
        for i in range(2):
            back(half - 1, NY - 1, i)
        return last()

    def only_back(tag, rhs, between):
        store, y_copy, send_batch, last = back_reducer(tag)

        def batch(k, _):
            for j in range(NY):
                for h, chunk in enumerate(chunks(k, j)):
                    store(k, j, h, jnp.dot(rhs[...], T[chunk], preferred_element_type=f32))
                if j < NY - 1:
                    y_copy(k, j).start()
            return 0

        lax.fori_loop(0, half, batch, 0)
        between()

        def sums(k, _):
            send_batch(k)
            return 0

        lax.fori_loop(0, half - 1, sums, 0)
        return last()

    def send_low():
        return [push(s["lo"].at[j], s["lr"].at[j], to_y[j]) for j in range(NY - 1)]

    def low_of(k, h, c):
        return sum(s["lr"][j, k, h, c].astype(f32) for j in range(NY - 1))

    def pass_low(copies):
        for copy in copies:
            copy.wait_recv()
        landing = []
        for d in range(1, nz):
            k, h = (d - half, 0) if d >= half else (half - 1 - d, 1)
            for c in range(2):
                s["zl"][d, c] = (s["tl"][d, c] + low_of(k, h, c)).astype(bf16)
            landing.append(push(s["zl"].at[d], s["zlr"].at[d], to_z[d - 1]))
        return landing

    def end_low(landing):
        value = [low_of(half - 1, 1, c) for c in range(2)]
        for d, copy in enumerate(landing):
            copy.wait_recv()
            value = [value[c] + s["zlr"][d + 1, c].astype(f32) for c in range(2)]
        return value

    def gather_forward(tag, value):
        G = s["G" + tag]
        base_z, base_y = take(nz), take(nz * (NY - 1))
        for c in range(2):
            G[y, z, c] = value[c].astype(bf16)

        def distance(i):
            return half + (2 * (i % 2) - 1) * (i // 2)

        def z_copy(i):
            return remote(G.at[y, z], G.at[y, z], at_z((z + distance(i)) % nz), base_z + i)

        def y_copy(i, zd, j):
            return remote(G.at[y, zd], G.at[y, zd], to_y[j], base_y + i * (NY - 1) + j)

        for i in range(1, nz):
            z_copy(i).start()
        for j in range(NY - 1):
            y_copy(0, z, j).start()
        acc[...] = jnp.zeros_like(acc)

        def pass_on(i, _):
            z_copy(i).wait_recv()
            for j in range(NY - 1):
                y_copy(i, (z - distance(i) + nz) % nz, j).start()
            return 0

        lax.fori_loop(1, nz, pass_on, 0)

        def forward(i, _):
            zd = jnp.where(i == 0, z, (z - distance(i) + nz) % nz)
            v = None
            for yd in range(NY):
                if yd < NY - 1:
                    y_copy(i, zd, yd).wait_recv()
            for yd in range(NY):
                g = jnp.concatenate([G[yd, zd, 0], G[yd, zd, 1]], axis=1)
                t = nt_dot(T[yd * nz + zd], g)
                v = t if v is None else v + t
            v = v.T
            for h in range(nf):
                acc[h] = acc[h] + v[:, 128 * h:128 * h + 128]
            return 0

        lax.fori_loop(0, nz, forward, 0)
        for i in range(nz):
            for j in range(NY - 1):
                pending.append(y_copy(i, z, j))
            if i:
                pending.append(z_copy(i))
        if tag == "b":
            ends.append(send_low())
        up, ur = s["up" + tag], s["ur" + tag]
        arriving = []
        for d in range(1, nf):
            to = (me + d) % nf
            up[d] = acc[to].astype(up.dtype)
            arriving.append(push(up.at[d], ur.at[d], at_f(to)))
        total = acc[me]
        for d, copy in enumerate(arriving):
            copy.wait_recv()
            total = total + ur[d + 1].astype(f32)
        slot = me * 128 + lax.broadcasted_iota(jnp.int32, (64, 128), 1)
        return jnp.where(slot < count, total, 0.0)

    def pack(tag, columns):
        at = lax.broadcasted_iota(jnp.int32, (64, 128), 1)
        tile = jnp.zeros((64, 128), f32)
        for k, v in enumerate(columns):
            tile = jnp.where(at == k, v, tile)
        s["sc" + tag][0, :, 0:64] = tile.T[0:8, :]

    def dots(pairs):
        return sum(jnp.sum(a * b, axis=1, keepdims=True) for a, b in pairs)

    def scalar_stage(tag, stage, targets):
        sc, sr = s["sc" + tag], s["sr%d" % stage + tag]
        copies = [push(sc.at[stage], sr.at[i], peer) for i, peer in enumerate(targets)]

        def finish():
            v = sc[stage]
            for i, copy in enumerate(copies):
                copy.wait_recv()
                v = v + sr[i]
            sc[stage + 1] = v

        return finish

    def unpack(tag, n):
        v = s["sc" + tag][len(STAGES[tag])]
        v = jnp.concatenate([v] * 16, axis=0).T
        return [v[0:64, k:k + 1] for k in range(n)]

    s["sca"][0] = jnp.zeros((8, 128), f32)
    s["scb"][0] = jnp.zeros((8, 128), f32)

    ends = []
    b = features_back("b")
    for c in range(2):
        s["bf"][c] = b[c]
    u = gather_forward("b", b)
    s["uf"][...] = u
    s["ui"][me] = u.astype(bf16)
    arriving = [push(s["ui"].at[me], s["ui"].at[me], peer) for peer in to_f]
    b = [s["bf"][c] for c in range(2)]
    pack("a", [dots([(b[0], b[0]), (b[1], b[1])]), dots([(u, u)])])
    finish = scalar_stage("a", 0, to_f)
    for copy in arriving:
        copy.wait_recv()
    for k in range(nf):
        s["yb"][:, 128 * k:128 * k + 128] = s["ui"][k]
    finish()
    finish = scalar_stage("a", 1, to_y)

    def between():
        finish()
        ends.append(scalar_stage("a", 2, to_z))
        ends.append(pass_low(ends[0]))

    g = only_back("g", s["yb"], between)
    ends[1]()
    low = end_low(ends[2])
    rr, uu = unpack("a", 2)
    alpha0 = rr / (uu + RIDGE * rr)
    b = [s["bf"][c] + low[c] for c in range(2)]
    r = [(1.0 - RIDGE * alpha0) * b[c] - alpha0 * g[c] for c in range(2)]
    for c in range(2):
        s["bf"][c] = b[c]
        s["rf"][c] = r[c]
    part = jnp.minimum(1.0, 2.0 * alpha0)
    v = gather_forward("g", [r[c] + part * (b[c] - s["Gb"][y, z, c].astype(f32)) for c in range(2)])
    u = s["uf"][...]
    b = [s["bf"][c] for c in range(2)]
    r = [s["rf"][c] for c in range(2)]
    pack("b", [dots([(r[0], r[0]), (r[1], r[1])]), dots([(r[0], b[0]), (r[1], b[1])]),
               dots([(v, v)]), dots([(v, u)])])
    scalar_stage("b", 0, to_yf)()
    scalar_stage("b", 1, to_z)()
    fresh, rb_, vv, vu = unpack("b", 4)
    rr, uu = unpack("a", 2)
    alpha0 = rr / (uu + RIDGE * rr)
    beta = fresh / rr
    image = vv + 2.0 * beta * vu + beta * beta * uu
    length = fresh + 2.0 * beta * rb_ + beta * beta * rr
    alpha1 = fresh / (image + RIDGE * length)
    on_b = jnp.broadcast_to(alpha0 + alpha1 * beta, (64, 128))
    on_r = jnp.broadcast_to(alpha1, (64, 128))

    def finish_chunk(k, _):
        at = pl.ds(pl.multiple_of(k * 128, 128), 128)
        for c in range(2):
            out_ref[c, :, at] = (on_b * s["Gb"][k // nz, k % nz, c].astype(f32)
                                 + on_r * s["Gg"][k // nz, k % nz, c].astype(f32))
        return 0

    lax.fori_loop(0, NY * nz, finish_chunk, 0)
    for copy in pending:
        copy.wait_send()


def per_device(nz, nf, inputs, freqs, targets, counts):
    rows, pairs = inputs.shape[0], freqs.shape[1]
    f32, bf16 = jnp.float32, jnp.bfloat16
    half = nz // 2
    copies = NY + nz + 2 * (half * (NY - 1) + 2 * nz + nz * (NY - 1) + nf - 1) + nf - 1 + (nf + NY + nz - 3) + (NY * nf + nz - 2)
    vmem = pltpu.VMEM
    scratch = {
        "T": vmem((NY * nz, rows, 256), bf16),
        "ph0": vmem((rows // 2, 256), f32),
        "ph1": vmem((rows // 2, 256), f32),
        "acc": vmem((nf, 64, 128), f32),
        "yb": vmem((64, rows), bf16),
        "bf": vmem((2, 64, 128), f32),
        "rf": vmem((2, 64, 128), f32),
        "uf": vmem((64, 128), f32),
        "ui": vmem((nf, 64, 128), bf16),
        "send": pltpu.SemaphoreType.DMA((copies,)),
        "recv": pltpu.SemaphoreType.DMA((copies,)),
    }
    for name, kind in (("lo", bf16), ("lr", bf16)):
        scratch[name] = vmem((NY - 1, half, 2, 2, 64, 128), kind)
    for name, kind in (("tl", f32), ("zl", bf16), ("zlr", bf16)):
        scratch[name] = vmem((nz, 2, 64, 128), kind)
    scratch["part"] = vmem((2, 2, 64, 128), f32)
    for tag in ("b", "g"):
        scratch["out" + tag] = vmem((NY - 1, half, 2, 2, 64, 128), bf16)
        scratch["own" + tag] = vmem((half, 2, 2, 64, 128), f32)
        scratch["r1" + tag] = vmem((NY - 1, half, 2, 2, 64, 128), bf16)
        scratch["tot" + tag] = vmem((nz, 2, 64, 128), bf16)
        scratch["zr" + tag] = vmem((nz, 2, 64, 128), bf16)
        scratch["G" + tag] = vmem((NY, nz, 2, 64, 128), bf16)
        scratch["up" + tag] = vmem((nf, 64, 128), bf16)
        scratch["ur" + tag] = vmem((nf, 64, 128), bf16)
    size = {"f": nf, "y": NY, "z": nz, "yf": NY * nf}
    for tag, stages in STAGES.items():
        scratch["sc" + tag] = vmem((len(stages) + 1, 8, 128), f32)
        for stage, group in enumerate(stages):
            scratch["sr%d" % stage + tag] = vmem((size[group], 8, 128), f32)
    whole = pl.BlockSpec(memory_space=pltpu.VMEM)
    out = pl.pallas_call(
        functools.partial(kernel, nz, nf, float(pairs * nf) ** -0.5),
        out_shape=jax.ShapeDtypeStruct((2, 64, pairs), f32),
        in_specs=[pl.BlockSpec(memory_space=pltpu.SMEM), whole, whole, whole],
        out_specs=whole,
        scratch_shapes=[scratch],
        compiler_params=pltpu.CompilerParams(
            collective_id=0, has_side_effects=True, vmem_limit_bytes=56 * 2 ** 20),
        cost_estimate=pl.CostEstimate(
            flops=12 * rows * pairs * 64, bytes_accessed=4 * 2 ** 20, transcendentals=0),
    )(counts, inputs, freqs, targets.T)
    return jnp.swapaxes(out, 1, 2)


def solution(mesh):
    nz, nf = mesh.shape["dp"] // NY, mesh.shape["freq"]
    return jax.shard_map(
        functools.partial(per_device, nz, nf),
        mesh=mesh,
        in_specs=(P("dp", None), P(None, "freq"), P("dp", None), P("dp")),
        out_specs=P(None, "freq", None),
        check_vma=False,
    )
```

```python
import functools
import math

import jax
import jax.numpy as jnp
from jax import lax
from jax.experimental import pallas as pl
from jax.experimental.pallas import tpu as pltpu
from jax.sharding import PartitionSpec as P

MESH = pl.DeviceIdType.MESH
RIDGE = 0.5
NY = 4
ROWT = 64
STAGES = {"a": ("f", "y", "z"), "b": ("yf", "z")}

SIN_HALF = (3.14158198, -5.1671413, 2.54188707, -0.554608852)
COS_HALF = (0.999999953, -4.93479283, 4.05841135, -1.33187657, 0.219689611)
INV_TURN = 0.15915494309189535


def nt_dot(a, b):
    return lax.dot_general(a, b, (((1,), (1,)), ((), ())), preferred_element_type=jnp.float32)


def cos_sin(phase, scale):
    gain = math.sqrt(2.0 * scale)
    turns = phase * INV_TURN
    frac = turns - jnp.round(turns)
    sq = frac * frac
    s = SIN_HALF[3] * gain
    for i in (2, 1, 0):
        s = s * sq + SIN_HALF[i] * gain
    c = COS_HALF[4] * gain
    for i in (3, 2, 1, 0):
        c = c * sq + COS_HALF[i] * gain
    s = s * frac
    return scale - s * s, s * c


def kernel(nz, nf, scale, count_ref, x_ref, w_ref, y_ref, out_ref, s):
    rows, half = 128 * nf, nz // 2
    rt = rows // 2
    f32, bf16 = jnp.float32, jnp.bfloat16
    dp, me = lax.axis_index("dp"), lax.axis_index("freq")
    z, y = dp // NY, dp % NY
    count = count_ref[0]
    T, acc = s["T"], s["acc"]

    def at_y(v):
        return (z * NY + v, me)

    def at_z(v):
        return (v * NY + y, me)

    def at_f(v):
        return (dp, v)

    to_f = [at_f((me + d) % nf) for d in range(1, nf)]
    to_y = [at_y((y + d) % NY) for d in range(1, NY)]
    to_z = [at_z((z + d) % nz) for d in range(1, nz)]
    to_yf = [(z * NY + (y + j) % NY, (me + d) % nf) for j in range(NY) for d in range(nf) if j + d]

    barrier = pltpu.get_barrier_semaphore()
    peers = to_yf + to_z
    for peer in peers:
        pl.semaphore_signal(barrier, inc=1, device_id=peer, device_id_type=MESH)

    pending = []
    used = [0]

    def take(n):
        used[0] += n
        return used[0] - n

    def remote(src, dst, peer, k):
        return pltpu.make_async_remote_copy(
            src_ref=src, dst_ref=dst, send_sem=s["send"].at[k], recv_sem=s["recv"].at[k],
            device_id=peer, device_id_type=MESH)

    def push(src, dst, peer):
        copy = remote(src, dst, peer, take(1))
        copy.start()
        pending.append(copy)
        return copy

    lane = lax.broadcasted_iota(jnp.int32, (64, rows), 1)
    s["yb"][...] = jnp.where(lane < count, y_ref[...].astype(f32), 0.0).astype(bf16)

    def chunks(k, j):
        yd = (y + 1 + j) % NY
        return yd * nz + (z + half + k) % nz, yd * nz + (z + half - 1 - k + nz) % nz

    def back_reducer(tag):
        out, own, r1, tot, zr = (s[k + tag] for k in ("out", "own", "r1", "tot", "zr"))
        base_y, base_z = take(half * (NY - 1)), take(nz)

        def store(k, j, h, v, more=True):
            for c in range(2):
                value = v[:, 128 * c:128 * c + 128]
                if tag == "b":
                    if more:
                        value = value + s["part"][h, c]
                    else:
                        s["part"][h, c] = value
                        continue
                if j == NY - 1:
                    own[k, h, c] = value
                    continue
                high = value.astype(bf16)
                out[j, k, h, c] = high
                if tag == "b":
                    s["lo"][j, k, h, c] = (value - high.astype(f32)).astype(bf16)

        def y_copy(k, j):
            return remote(out.at[j, k], r1.at[j, k], to_y[j], base_y + k * (NY - 1) + j)

        def z_copy(d):
            return remote(tot.at[d], zr.at[d], at_z((z + d) % nz), base_z + d)

        def sum_y(k, h):
            v = [own[k, h, c] for c in range(2)]
            for j in range(NY - 1):
                v = [v[c] + r1[j, k, h, c].astype(f32) for c in range(2)]
            return v

        def send_z(k, h, d):
            for c, v in enumerate(sum_y(k, h)):
                high = v.astype(bf16)
                tot[d, c] = high
                if tag == "b":
                    s["tl"][d, c] = v - high.astype(f32)
            z_copy(d).start()

        def wait_y(k):
            for j in range(NY - 1):
                y_copy(k, j).wait_recv()

        def send_batch(k):
            wait_y(k)
            send_z(k, 0, half + k)
            send_z(k, 1, half - 1 - k)

        def last():
            wait_y(half - 1)
            send_z(half - 1, 0, nz - 1)
            value = sum_y(half - 1, 1)
            for d in range(1, nz):
                z_copy(d).wait_recv()
                value = [value[c] + zr[d, c].astype(f32) for c in range(2)]
            for k in range(half):
                for j in range(NY - 1):
                    pending.append(y_copy(k, j))
            for d in range(1, nz):
                pending.append(z_copy(d))
            return value

        return store, y_copy, send_batch, last

    def features_back(tag):
        store, y_copy, send_batch, last = back_reducer(tag)
        phases = (s["ph0"], s["ph1"])

        def phase(k, j, i):
            w = [w_ref[:, pl.ds(pl.multiple_of(c * 128, 128), 128)] for c in chunks(k, j)]
            return jnp.dot(x_ref[rt * i:rt * i + rt, :], jnp.concatenate(w, axis=1),
                           preferred_element_type=f32)

        def back(k, j, i):
            for h, chunk in enumerate(chunks(k, j)):
                v = jnp.dot(s["yb"][:, rt * i:rt * i + rt], T[chunk, rt * i:rt * i + rt, :],
                            preferred_element_type=f32)
                store(k, j, h, v, i > 0)

        for chunk in chunks(0, NY - 1):
            T[chunk] = jnp.zeros((rows, 256), bf16)
        phases[0][...] = phase(0, 0, 0)

        def batch(k, _):
            for j in range(NY):
                pk, pj = (k, j - 1) if j else (jnp.maximum(k - 1, 0), NY - 1)
                nk, nj = (k, j + 1) if j < NY - 1 else ((k + 1) % half, 0)
                here = chunks(k, j)
                for i in range(2):
                    back(pk, pj, i)
                    phases[1 - i][...] = phase(k, j, 1) if i == 0 else phase(nk, nj, 0)
                    for r in range(0, rt, ROWT):
                        c, v = cos_sin(phases[i][r:r + ROWT, :], scale)
                        c, v = c.astype(bf16), v.astype(bf16)
                        for h in range(2):
                            at = pl.ds(rt * i + r, ROWT)
                            T[here[h], at, 0:128] = c[:, 128 * h:128 * h + 128]
                            T[here[h], at, 128:256] = v[:, 128 * h:128 * h + 128]
                if j == 1:
                    @pl.when(k == 0)
                    def _():
                        pl.semaphore_wait(barrier, len(peers))
                if j:
                    y_copy(k, j - 1).start()
            pl.when(k > 0)(lambda: send_batch(k - 1))
            return 0

        lax.fori_loop(0, half, batch, 0)
        for i in range(2):
            back(half - 1, NY - 1, i)
        ends.append(send_low())
        return last()

    def only_back(tag, rhs, between):
        store, y_copy, send_batch, last = back_reducer(tag)

        def batch(k, _):
            for j in range(NY):
                for h, chunk in enumerate(chunks(k, j)):
                    store(k, j, h, jnp.dot(rhs[...], T[chunk], preferred_element_type=f32))
                if j < NY - 1:
                    y_copy(k, j).start()
            return 0

        lax.fori_loop(0, half, batch, 0)
        between()

        def sums(k, _):
            send_batch(k)
            return 0

        lax.fori_loop(0, half - 1, sums, 0)
        return last()

    def send_low():
        return [push(s["lo"].at[j], s["lr"].at[j], to_y[j]) for j in range(NY - 1)]

    def low_of(k, h, c):
        return sum(s["lr"][j, k, h, c].astype(f32) for j in range(NY - 1))

    def pass_low(copies):
        for copy in copies:
            copy.wait_recv()
        landing = []
        for d in range(1, nz):
            k, h = (d - half, 0) if d >= half else (half - 1 - d, 1)
            for c in range(2):
                s["zl"][d, c] = (s["tl"][d, c] + low_of(k, h, c)).astype(bf16)
            landing.append(push(s["zl"].at[d], s["zlr"].at[d], to_z[d - 1]))
        return landing

    def end_low(landing):
        value = [low_of(half - 1, 1, c) for c in range(2)]
        for d, copy in enumerate(landing):
            copy.wait_recv()
            value = [value[c] + s["zlr"][d + 1, c].astype(f32) for c in range(2)]
        return value

    def gather_forward(tag, value):
        G = s["G" + tag]
        base_z, base_y = take(nz), take(nz * (NY - 1))
        for c in range(2):
            G[y, z, c] = value[c].astype(bf16)

        def distance(i):
            return half + (2 * (i % 2) - 1) * (i // 2)

        def z_copy(i):
            return remote(G.at[y, z], G.at[y, z], at_z((z + distance(i)) % nz), base_z + i)

        def y_copy(i, zd, j):
            return remote(G.at[y, zd], G.at[y, zd], to_y[j], base_y + i * (NY - 1) + j)

        for i in range(1, nz):
            z_copy(i).start()
        for j in range(NY - 1):
            y_copy(0, z, j).start()
        acc[...] = jnp.zeros_like(acc)

        def pass_on(i, _):
            z_copy(i).wait_recv()
            for j in range(NY - 1):
                y_copy(i, (z - distance(i) + nz) % nz, j).start()
            return 0

        lax.fori_loop(1, nz, pass_on, 0)

        def forward(i, _):
            zd = jnp.where(i == 0, z, (z - distance(i) + nz) % nz)
            v = None
            for yd in range(NY):
                if yd < NY - 1:
                    y_copy(i, zd, yd).wait_recv()
            for yd in range(NY):
                g = jnp.concatenate([G[yd, zd, 0], G[yd, zd, 1]], axis=1)
                t = nt_dot(T[yd * nz + zd], g)
                v = t if v is None else v + t
            v = v.T
            for h in range(nf):
                acc[h] = acc[h] + v[:, 128 * h:128 * h + 128]
            return 0

        lax.fori_loop(0, nz, forward, 0)
        for i in range(nz):
            for j in range(NY - 1):
                pending.append(y_copy(i, z, j))
            if i:
                pending.append(z_copy(i))
        up, ur = s["up" + tag], s["ur" + tag]
        arriving = []
        for d in range(1, nf):
            to = (me + d) % nf
            up[d] = acc[to].astype(up.dtype)
            arriving.append(push(up.at[d], ur.at[d], at_f(to)))
        if tag == "b":
            ends.append(pass_low(ends[0]))
        total = acc[me]
        for d, copy in enumerate(arriving):
            copy.wait_recv()
            total = total + ur[d + 1].astype(f32)
        slot = me * 128 + lax.broadcasted_iota(jnp.int32, (64, 128), 1)
        return jnp.where(slot < count, total, 0.0)

    def pack(tag, columns):
        at = lax.broadcasted_iota(jnp.int32, (64, 128), 1)
        tile = jnp.zeros((64, 128), f32)
        for k, v in enumerate(columns):
            tile = jnp.where(at == k, v, tile)
        s["sc" + tag][0, :, 0:64] = tile.T[0:8, :]

    def dots(pairs):
        return sum(jnp.sum(a * b, axis=1, keepdims=True) for a, b in pairs)

    def scalar_stage(tag, stage, targets):
        sc, sr = s["sc" + tag], s["sr%d" % stage + tag]
        copies = [push(sc.at[stage], sr.at[i], peer) for i, peer in enumerate(targets)]

        def finish():
            v = sc[stage]
            for i, copy in enumerate(copies):
                copy.wait_recv()
                v = v + sr[i]
            sc[stage + 1] = v

        return finish

    def unpack(tag, n):
        v = s["sc" + tag][len(STAGES[tag])]
        v = jnp.concatenate([v] * 16, axis=0).T
        return [v[0:64, k:k + 1] for k in range(n)]

    s["sca"][0] = jnp.zeros((8, 128), f32)
    s["scb"][0] = jnp.zeros((8, 128), f32)

    ends = []
    b = features_back("b")
    for c in range(2):
        s["bf"][c] = b[c]
    u = gather_forward("b", b)
    s["uf"][...] = u
    s["ui"][me] = u.astype(bf16)
    arriving = [push(s["ui"].at[me], s["ui"].at[me], peer) for peer in to_f]
    b = [s["bf"][c] for c in range(2)]
    pack("a", [dots([(b[0], b[0]), (b[1], b[1])]), dots([(u, u)])])
    finish = scalar_stage("a", 0, to_f)
    for copy in arriving:
        copy.wait_recv()
    for k in range(nf):
        s["yb"][:, 128 * k:128 * k + 128] = s["ui"][k]
    finish()
    finish = scalar_stage("a", 1, to_y)

    def between():
        finish()
        ends.append(scalar_stage("a", 2, to_z))

    g = only_back("g", s["yb"], between)
    ends[2]()
    low = end_low(ends[1])
    rr, uu = unpack("a", 2)
    alpha0 = rr / (uu + RIDGE * rr)
    b = [s["bf"][c] + low[c] for c in range(2)]
    r = [(1.0 - RIDGE * alpha0) * b[c] - alpha0 * g[c] for c in range(2)]
    for c in range(2):
        s["bf"][c] = b[c]
        s["rf"][c] = r[c]
    part = jnp.minimum(1.0, 2.0 * alpha0)
    v = gather_forward("g", [r[c] + part * (b[c] - s["Gb"][y, z, c].astype(f32)) for c in range(2)])
    u = s["uf"][...]
    b = [s["bf"][c] for c in range(2)]
    r = [s["rf"][c] for c in range(2)]
    pack("b", [dots([(r[0], r[0]), (r[1], r[1])]), dots([(r[0], b[0]), (r[1], b[1])]),
               dots([(v, v)]), dots([(v, u)])])
    scalar_stage("b", 0, to_yf)()
    scalar_stage("b", 1, to_z)()
    fresh, rb_, vv, vu = unpack("b", 4)
    rr, uu = unpack("a", 2)
    alpha0 = rr / (uu + RIDGE * rr)
    beta = fresh / rr
    image = vv + 2.0 * beta * vu + beta * beta * uu
    length = fresh + 2.0 * beta * rb_ + beta * beta * rr
    alpha1 = fresh / (image + RIDGE * length)
    on_b = jnp.broadcast_to(alpha0 + alpha1 * beta, (64, 128))
    on_r = jnp.broadcast_to(alpha1, (64, 128))

    def finish_chunk(k, _):
        at = pl.ds(pl.multiple_of(k * 128, 128), 128)
        for c in range(2):
            out_ref[c, :, at] = (on_b * s["Gb"][k // nz, k % nz, c].astype(f32)
                                 + on_r * s["Gg"][k // nz, k % nz, c].astype(f32))
        return 0

    lax.fori_loop(0, NY * nz, finish_chunk, 0)
    for copy in pending:
        copy.wait_send()


def per_device(nz, nf, inputs, freqs, targets, counts):
    rows, pairs = inputs.shape[0], freqs.shape[1]
    f32, bf16 = jnp.float32, jnp.bfloat16
    half = nz // 2
    copies = NY + nz + 2 * (half * (NY - 1) + 2 * nz + nz * (NY - 1) + nf - 1) + nf - 1 + (nf + NY + nz - 3) + (NY * nf + nz - 2)
    vmem = pltpu.VMEM
    scratch = {
        "T": vmem((NY * nz, rows, 256), bf16),
        "ph0": vmem((rows // 2, 256), f32),
        "ph1": vmem((rows // 2, 256), f32),
        "acc": vmem((nf, 64, 128), f32),
        "yb": vmem((64, rows), bf16),
        "bf": vmem((2, 64, 128), f32),
        "rf": vmem((2, 64, 128), f32),
        "uf": vmem((64, 128), f32),
        "ui": vmem((nf, 64, 128), bf16),
        "send": pltpu.SemaphoreType.DMA((copies,)),
        "recv": pltpu.SemaphoreType.DMA((copies,)),
    }
    for name, kind in (("lo", bf16), ("lr", bf16)):
        scratch[name] = vmem((NY - 1, half, 2, 2, 64, 128), kind)
    for name, kind in (("tl", f32), ("zl", bf16), ("zlr", bf16)):
        scratch[name] = vmem((nz, 2, 64, 128), kind)
    scratch["part"] = vmem((2, 2, 64, 128), f32)
    for tag in ("b", "g"):
        scratch["out" + tag] = vmem((NY - 1, half, 2, 2, 64, 128), bf16)
        scratch["own" + tag] = vmem((half, 2, 2, 64, 128), f32)
        scratch["r1" + tag] = vmem((NY - 1, half, 2, 2, 64, 128), bf16)
        scratch["tot" + tag] = vmem((nz, 2, 64, 128), bf16)
        scratch["zr" + tag] = vmem((nz, 2, 64, 128), bf16)
        scratch["G" + tag] = vmem((NY, nz, 2, 64, 128), bf16)
        scratch["up" + tag] = vmem((nf, 64, 128), bf16)
        scratch["ur" + tag] = vmem((nf, 64, 128), bf16)
    size = {"f": nf, "y": NY, "z": nz, "yf": NY * nf}
    for tag, stages in STAGES.items():
        scratch["sc" + tag] = vmem((len(stages) + 1, 8, 128), f32)
        for stage, group in enumerate(stages):
            scratch["sr%d" % stage + tag] = vmem((size[group], 8, 128), f32)
    whole = pl.BlockSpec(memory_space=pltpu.VMEM)
    out = pl.pallas_call(
        functools.partial(kernel, nz, nf, float(pairs * nf) ** -0.5),
        out_shape=jax.ShapeDtypeStruct((2, 64, pairs), f32),
        in_specs=[pl.BlockSpec(memory_space=pltpu.SMEM), whole, whole, whole],
        out_specs=whole,
        scratch_shapes=[scratch],
        compiler_params=pltpu.CompilerParams(
            collective_id=0, has_side_effects=True, vmem_limit_bytes=56 * 2 ** 20),
        cost_estimate=pl.CostEstimate(
            flops=12 * rows * pairs * 64, bytes_accessed=4 * 2 ** 20, transcendentals=0),
    )(counts, inputs, freqs, targets.T)
    return jnp.swapaxes(out, 1, 2)


def solution(mesh):
    nz, nf = mesh.shape["dp"] // NY, mesh.shape["freq"]
    return jax.shard_map(
        functools.partial(per_device, nz, nf),
        mesh=mesh,
        in_specs=(P("dp", None), P(None, "freq"), P("dp", None), P("dp")),
        out_specs=P(None, "freq", None),
        check_vma=False,
    )
```

```python
import functools
import math

import jax
import jax.numpy as jnp
from jax import lax
from jax.experimental import pallas as pl
from jax.experimental.pallas import tpu as pltpu
from jax.sharding import PartitionSpec as P

MESH = pl.DeviceIdType.MESH
RIDGE = 0.5
NY = 4
ROWT = 64
STAGES = {"a": ("f", "y", "z"), "b": ("yf", "z")}

SIN_HALF = (3.14158198, -5.1671413, 2.54188707, -0.554608852)
COS_HALF = (0.999999953, -4.93479283, 4.05841135, -1.33187657, 0.219689611)
INV_TURN = 0.15915494309189535


def nt_dot(a, b):
    return lax.dot_general(a, b, (((1,), (1,)), ((), ())), preferred_element_type=jnp.float32)


def cos_sin(phase, scale):
    gain = math.sqrt(2.0 * scale)
    turns = phase * INV_TURN
    frac = turns - jnp.round(turns)
    sq = frac * frac
    s = SIN_HALF[3] * gain
    for i in (2, 1, 0):
        s = s * sq + SIN_HALF[i] * gain
    c = COS_HALF[4] * gain
    for i in (3, 2, 1, 0):
        c = c * sq + COS_HALF[i] * gain
    s = s * frac
    return scale - s * s, s * c


def kernel(nz, nf, scale, count_ref, x_ref, w_ref, y_ref, out_ref, s):
    rows, half = 128 * nf, nz // 2
    rt = rows // 2
    f32, bf16 = jnp.float32, jnp.bfloat16
    dp, me = lax.axis_index("dp"), lax.axis_index("freq")
    z, y = dp // NY, dp % NY
    count = count_ref[0]
    T, acc = s["T"], s["acc"]

    def at_y(v):
        return (z * NY + v, me)

    def at_z(v):
        return (v * NY + y, me)

    def at_f(v):
        return (dp, v)

    to_f = [at_f((me + d) % nf) for d in range(1, nf)]
    to_y = [at_y((y + d) % NY) for d in range(1, NY)]
    to_z = [at_z((z + d) % nz) for d in range(1, nz)]
    to_yf = [(z * NY + (y + j) % NY, (me + d) % nf) for j in range(NY) for d in range(nf) if j + d]

    barrier = pltpu.get_barrier_semaphore()
    peers = to_yf + to_z
    for peer in peers:
        pl.semaphore_signal(barrier, inc=1, device_id=peer, device_id_type=MESH)

    pending = []
    used = [0]

    def take(n):
        used[0] += n
        return used[0] - n

    def remote(src, dst, peer, k):
        return pltpu.make_async_remote_copy(
            src_ref=src, dst_ref=dst, send_sem=s["send"].at[k], recv_sem=s["recv"].at[k],
            device_id=peer, device_id_type=MESH)

    def push(src, dst, peer):
        copy = remote(src, dst, peer, take(1))
        copy.start()
        pending.append(copy)
        return copy

    lane = lax.broadcasted_iota(jnp.int32, (64, rows), 1)
    s["yb"][...] = jnp.where(lane < count, y_ref[...].astype(f32), 0.0).astype(bf16)

    def chunks(k, j):
        yd = (y + 1 + j) % NY
        return yd * nz + (z + half + k) % nz, yd * nz + (z + half - 1 - k + nz) % nz

    def back_reducer(tag):
        out, own, r1, tot, zr = (s[k + tag] for k in ("out", "own", "r1", "tot", "zr"))
        base_y, base_z = take(half * (NY - 1)), take(nz)

        def store(k, j, h, v, more=True):
            for c in range(2):
                value = v[:, 128 * c:128 * c + 128]
                if tag == "b":
                    if more:
                        value = value + s["part"][h, c]
                    else:
                        s["part"][h, c] = value
                        continue
                if j == NY - 1:
                    own[k, h, c] = value
                    continue
                high = value.astype(bf16)
                out[j, k, h, c] = high
                if tag == "b":
                    s["lo"][j, k, h, c] = (value - high.astype(f32)).astype(bf16)

        def y_copy(k, j):
            return remote(out.at[j, k], r1.at[j, k], to_y[j], base_y + k * (NY - 1) + j)

        def z_copy(d):
            return remote(tot.at[d], zr.at[d], at_z((z + d) % nz), base_z + d)

        def sum_y(k, h):
            v = [own[k, h, c] for c in range(2)]
            for j in range(NY - 1):
                v = [v[c] + r1[j, k, h, c].astype(f32) for c in range(2)]
            return v

        def send_z(k, h, d):
            for c, v in enumerate(sum_y(k, h)):
                high = v.astype(bf16)
                tot[d, c] = high
                if tag == "b":
                    s["tl"][d, c] = v - high.astype(f32)
            z_copy(d).start()

        def wait_y(k):
            for j in range(NY - 1):
                y_copy(k, j).wait_recv()

        def send_batch(k):
            wait_y(k)
            send_z(k, 0, half + k)
            send_z(k, 1, half - 1 - k)

        def last():
            wait_y(half - 1)
            send_z(half - 1, 0, nz - 1)
            value = sum_y(half - 1, 1)
            for d in range(1, nz):
                z_copy(d).wait_recv()
                value = [value[c] + zr[d, c].astype(f32) for c in range(2)]
            for k in range(half):
                for j in range(NY - 1):
                    pending.append(y_copy(k, j))
            for d in range(1, nz):
                pending.append(z_copy(d))
            return value

        return store, y_copy, send_batch, last

    def features_back(tag):
        store, y_copy, send_batch, last = back_reducer(tag)
        phases = (s["ph0"], s["ph1"])

        def phase(k, j, i):
            w = [w_ref[:, pl.ds(pl.multiple_of(c * 128, 128), 128)] for c in chunks(k, j)]
            return jnp.dot(x_ref[rt * i:rt * i + rt, :], jnp.concatenate(w, axis=1),
                           preferred_element_type=f32)

        def back(k, j, i):
            for h, chunk in enumerate(chunks(k, j)):
                v = jnp.dot(s["yb"][:, rt * i:rt * i + rt], T[chunk, rt * i:rt * i + rt, :],
                            preferred_element_type=f32)
                store(k, j, h, v, i > 0)

        for chunk in chunks(0, NY - 1):
            T[chunk] = jnp.zeros((rows, 256), bf16)
        phases[0][...] = phase(0, 0, 0)

        def batch(k, _):
            for j in range(NY):
                pk, pj = (k, j - 1) if j else (jnp.maximum(k - 1, 0), NY - 1)
                nk, nj = (k, j + 1) if j < NY - 1 else ((k + 1) % half, 0)
                here = chunks(k, j)
                for i in range(2):
                    back(pk, pj, i)
                    phases[1 - i][...] = phase(k, j, 1) if i == 0 else phase(nk, nj, 0)
                    for r in range(0, rt, ROWT):
                        c, v = cos_sin(phases[i][r:r + ROWT, :], scale)
                        c, v = c.astype(bf16), v.astype(bf16)
                        for h in range(2):
                            at = pl.ds(rt * i + r, ROWT)
                            T[here[h], at, 0:128] = c[:, 128 * h:128 * h + 128]
                            T[here[h], at, 128:256] = v[:, 128 * h:128 * h + 128]
                if j == 1:
                    @pl.when(k == 0)
                    def _():
                        pl.semaphore_wait(barrier, len(peers))
                if j:
                    y_copy(k, j - 1).start()
            pl.when(k > 0)(lambda: send_batch(k - 1))
            return 0

        lax.fori_loop(0, half, batch, 0)
        for i in range(2):
            back(half - 1, NY - 1, i)
        ends.append(send_low())
        return last()

    def only_back(tag, rhs, between):
        store, y_copy, send_batch, last = back_reducer(tag)

        def batch(k, _):
            for j in range(NY):
                for h, chunk in enumerate(chunks(k, j)):
                    store(k, j, h, jnp.dot(rhs[...], T[chunk], preferred_element_type=f32))
                if j < NY - 1:
                    y_copy(k, j).start()
            return 0

        lax.fori_loop(0, half, batch, 0)
        between()

        def sums(k, _):
            send_batch(k)
            return 0

        lax.fori_loop(0, half - 1, sums, 0)
        return last()

    def send_low():
        return [push(s["lo"].at[j], s["lr"].at[j], to_y[j]) for j in range(NY - 1)]

    def low_of(k, h, c):
        return sum(s["lr"][j, k, h, c].astype(f32) for j in range(NY - 1))

    def pass_low(copies):
        for copy in copies:
            copy.wait_recv()
        landing = []
        for d in range(1, nz):
            k, h = (d - half, 0) if d >= half else (half - 1 - d, 1)
            for c in range(2):
                s["zl"][d, c] = (s["tl"][d, c] + low_of(k, h, c)).astype(bf16)
            landing.append(push(s["zl"].at[d], s["zlr"].at[d], to_z[d - 1]))
        return landing

    def end_low(landing):
        value = [low_of(half - 1, 1, c) for c in range(2)]
        for d, copy in enumerate(landing):
            copy.wait_recv()
            value = [value[c] + s["zlr"][d + 1, c].astype(f32) for c in range(2)]
        return value

    def gather_forward(tag, value):
        G = s["G" + tag]
        base_z, base_y = take(nz), take(nz * (NY - 1))
        for c in range(2):
            G[y, z, c] = value[c].astype(bf16)

        def distance(i):
            return (i % 2) * ((i + 1) // 2) + (1 - i % 2) * (nz - i // 2)

        def z_copy(i):
            return remote(G.at[y, z], G.at[y, z], at_z((z + distance(i)) % nz), base_z + i)

        def y_copy(i, zd, j):
            return remote(G.at[y, zd], G.at[y, zd], to_y[j], base_y + i * (NY - 1) + j)

        for i in (nz - 1, *range(1, nz - 1)):
            z_copy(i).start()
        for j in range(NY - 1):
            y_copy(0, z, j).start()
        acc[...] = jnp.zeros_like(acc)

        def pass_on(i, _):
            z_copy(i).wait_recv()
            for j in range(NY - 1):
                y_copy(i, (z - distance(i) + nz) % nz, j).start()
            return 0

        lax.fori_loop(1, nz, pass_on, 0)

        def forward(i, _):
            zd = jnp.where(i == 0, z, (z - distance(i) + nz) % nz)
            v = None
            for yd in range(NY):
                if yd < NY - 1:
                    y_copy(i, zd, yd).wait_recv()
            for yd in range(NY):
                g = jnp.concatenate([G[yd, zd, 0], G[yd, zd, 1]], axis=1)
                t = nt_dot(T[yd * nz + zd], g)
                v = t if v is None else v + t
            v = v.T
            for h in range(nf):
                acc[h] = acc[h] + v[:, 128 * h:128 * h + 128]
            return 0

        lax.fori_loop(0, nz, forward, 0)
        for i in range(nz):
            for j in range(NY - 1):
                pending.append(y_copy(i, z, j))
            if i:
                pending.append(z_copy(i))
        up, ur = s["up" + tag], s["ur" + tag]
        arriving = []
        for d in range(1, nf):
            to = (me + d) % nf
            up[d] = acc[to].astype(up.dtype)
            arriving.append(push(up.at[d], ur.at[d], at_f(to)))
        if tag == "b":
            ends.append(pass_low(ends[0]))
        total = acc[me]
        for d, copy in enumerate(arriving):
            copy.wait_recv()
            total = total + ur[d + 1].astype(f32)
        slot = me * 128 + lax.broadcasted_iota(jnp.int32, (64, 128), 1)
        return jnp.where(slot < count, total, 0.0)

    def pack(tag, columns):
        at = lax.broadcasted_iota(jnp.int32, (64, 128), 1)
        tile = jnp.zeros((64, 128), f32)
        for k, v in enumerate(columns):
            tile = jnp.where(at == k, v, tile)
        s["sc" + tag][0, :, 0:64] = tile.T[0:8, :]

    def dots(pairs):
        return sum(jnp.sum(a * b, axis=1, keepdims=True) for a, b in pairs)

    def scalar_stage(tag, stage, targets):
        sc, sr = s["sc" + tag], s["sr%d" % stage + tag]
        copies = [push(sc.at[stage], sr.at[i], peer) for i, peer in enumerate(targets)]

        def finish():
            v = sc[stage]
            for i, copy in enumerate(copies):
                copy.wait_recv()
                v = v + sr[i]
            sc[stage + 1] = v

        return finish

    def unpack(tag, n):
        v = s["sc" + tag][len(STAGES[tag])]
        v = jnp.concatenate([v] * 16, axis=0).T
        return [v[0:64, k:k + 1] for k in range(n)]

    s["sca"][0] = jnp.zeros((8, 128), f32)
    s["scb"][0] = jnp.zeros((8, 128), f32)

    ends = []
    b = features_back("b")
    for c in range(2):
        s["bf"][c] = b[c]
    u = gather_forward("b", b)
    s["uf"][...] = u
    s["ui"][me] = u.astype(bf16)
    arriving = [push(s["ui"].at[me], s["ui"].at[me], peer) for peer in to_f]
    b = [s["bf"][c] for c in range(2)]
    pack("a", [dots([(b[0], b[0]), (b[1], b[1])]), dots([(u, u)])])
    finish = scalar_stage("a", 0, to_f)
    for copy in arriving:
        copy.wait_recv()
    for k in range(nf):
        s["yb"][:, 128 * k:128 * k + 128] = s["ui"][k]
    finish()
    finish = scalar_stage("a", 1, to_y)

    def between():
        finish()
        ends.append(scalar_stage("a", 2, to_z))

    g = only_back("g", s["yb"], between)
    ends[2]()
    low = end_low(ends[1])
    rr, uu = unpack("a", 2)
    alpha0 = rr / (uu + RIDGE * rr)
    b = [s["bf"][c] + low[c] for c in range(2)]
    r = [(1.0 - RIDGE * alpha0) * b[c] - alpha0 * g[c] for c in range(2)]
    for c in range(2):
        s["bf"][c] = b[c]
        s["rf"][c] = r[c]
    part = jnp.minimum(1.0, 2.0 * alpha0)
    v = gather_forward("g", [r[c] + part * (b[c] - s["Gb"][y, z, c].astype(f32)) for c in range(2)])
    u = s["uf"][...]
    b = [s["bf"][c] for c in range(2)]
    r = [s["rf"][c] for c in range(2)]
    pack("b", [dots([(r[0], r[0]), (r[1], r[1])]), dots([(r[0], b[0]), (r[1], b[1])]),
               dots([(v, v)]), dots([(v, u)])])
    scalar_stage("b", 0, to_yf)()
    scalar_stage("b", 1, to_z)()
    fresh, rb_, vv, vu = unpack("b", 4)
    rr, uu = unpack("a", 2)
    alpha0 = rr / (uu + RIDGE * rr)
    beta = fresh / rr
    image = vv + 2.0 * beta * vu + beta * beta * uu
    length = fresh + 2.0 * beta * rb_ + beta * beta * rr
    alpha1 = fresh / (image + RIDGE * length)
    on_b = jnp.broadcast_to(alpha0 + alpha1 * beta, (64, 128))
    on_r = jnp.broadcast_to(alpha1, (64, 128))

    def finish_chunk(k, _):
        at = pl.ds(pl.multiple_of(k * 128, 128), 128)
        for c in range(2):
            out_ref[c, :, at] = (on_b * s["Gb"][k // nz, k % nz, c].astype(f32)
                                 + on_r * s["Gg"][k // nz, k % nz, c].astype(f32))
        return 0

    lax.fori_loop(0, NY * nz, finish_chunk, 0)
    for copy in pending:
        copy.wait_send()


def per_device(nz, nf, inputs, freqs, targets, counts):
    rows, pairs = inputs.shape[0], freqs.shape[1]
    f32, bf16 = jnp.float32, jnp.bfloat16
    half = nz // 2
    copies = NY + nz + 2 * (half * (NY - 1) + 2 * nz + nz * (NY - 1) + nf - 1) + nf - 1 + (nf + NY + nz - 3) + (NY * nf + nz - 2)
    vmem = pltpu.VMEM
    scratch = {
        "T": vmem((NY * nz, rows, 256), bf16),
        "ph0": vmem((rows // 2, 256), f32),
        "ph1": vmem((rows // 2, 256), f32),
        "acc": vmem((nf, 64, 128), f32),
        "yb": vmem((64, rows), bf16),
        "bf": vmem((2, 64, 128), f32),
        "rf": vmem((2, 64, 128), f32),
        "uf": vmem((64, 128), f32),
        "ui": vmem((nf, 64, 128), bf16),
        "send": pltpu.SemaphoreType.DMA((copies,)),
        "recv": pltpu.SemaphoreType.DMA((copies,)),
    }
    for name, kind in (("lo", bf16), ("lr", bf16)):
        scratch[name] = vmem((NY - 1, half, 2, 2, 64, 128), kind)
    for name, kind in (("tl", f32), ("zl", bf16), ("zlr", bf16)):
        scratch[name] = vmem((nz, 2, 64, 128), kind)
    scratch["part"] = vmem((2, 2, 64, 128), f32)
    for tag in ("b", "g"):
        scratch["out" + tag] = vmem((NY - 1, half, 2, 2, 64, 128), bf16)
        scratch["own" + tag] = vmem((half, 2, 2, 64, 128), f32)
        scratch["r1" + tag] = vmem((NY - 1, half, 2, 2, 64, 128), bf16)
        scratch["tot" + tag] = vmem((nz, 2, 64, 128), bf16)
        scratch["zr" + tag] = vmem((nz, 2, 64, 128), bf16)
        scratch["G" + tag] = vmem((NY, nz, 2, 64, 128), bf16)
        scratch["up" + tag] = vmem((nf, 64, 128), bf16)
        scratch["ur" + tag] = vmem((nf, 64, 128), bf16)
    size = {"f": nf, "y": NY, "z": nz, "yf": NY * nf}
    for tag, stages in STAGES.items():
        scratch["sc" + tag] = vmem((len(stages) + 1, 8, 128), f32)
        for stage, group in enumerate(stages):
            scratch["sr%d" % stage + tag] = vmem((size[group], 8, 128), f32)
    whole = pl.BlockSpec(memory_space=pltpu.VMEM)
    out = pl.pallas_call(
        functools.partial(kernel, nz, nf, float(pairs * nf) ** -0.5),
        out_shape=jax.ShapeDtypeStruct((2, 64, pairs), f32),
        in_specs=[pl.BlockSpec(memory_space=pltpu.SMEM), whole, whole, whole],
        out_specs=whole,
        scratch_shapes=[scratch],
        compiler_params=pltpu.CompilerParams(
            collective_id=0, has_side_effects=True, vmem_limit_bytes=56 * 2 ** 20),
        cost_estimate=pl.CostEstimate(
            flops=12 * rows * pairs * 64, bytes_accessed=4 * 2 ** 20, transcendentals=0),
    )(counts, inputs, freqs, targets.T)
    return jnp.swapaxes(out, 1, 2)


def solution(mesh):
    nz, nf = mesh.shape["dp"] // NY, mesh.shape["freq"]
    return jax.shard_map(
        functools.partial(per_device, nz, nf),
        mesh=mesh,
        in_specs=(P("dp", None), P(None, "freq"), P("dp", None), P("dp")),
        out_specs=P(None, "freq", None),
        check_vma=False,
    )
```
